128 devices in a mesh: blk: 8 (over x, core), ma: 16 (over y, z).
Axes of the slice: x: 4, y: 4, z: 4, core: 2. Of those that a mesh axis runs over, the one named last changes fastest.
Arguments:
- solution: float32 [64, 8, 4, 4096], P('ma', None, None, 'blk'), may hold values from -6 to 6
- residual: float32 [64, 8, 4, 4096], P('ma', None, None, 'blk'), may hold values from -6 to 6
- direction: float32 [64, 8, 4, 4096], P('ma', None, None, 'blk'), may hold values from -6 to 6
- legendre: bfloat16 [64, 2, 2048, 4096], P('ma', None, 'blk'), may hold values from -0.09375 to 0.09375
- prior_inverse: float32 [2, 8, 8, 4096], P(None, None, None, 'blk'), may hold values from -0.15 to 4, as said below
- inverse_noise: bfloat16 [2048, 8, 16384], P(('blk', 'ma')), may hold values from 0.25 to 4
- cycle_length: int32 [2048], P(('blk', 'ma')), may hold values from 4 to 16384, as said below
- order_list: int32 [64], replicated, may hold values from 0 to 4096, as said below
Outputs:
- solution_next: float32 [64, 8, 4, 4096], P('ma', None, None, 'blk')
- residual_next: float32 [64, 8, 4, 4096], P('ma', None, None, 'blk')
- direction_next: float32 [64, 8, 4, 4096], P('ma', None, None, 'blk')
The draws below stay inside these ranges and needn't reach their ends.
Inputs may be any that keep to these rules, and one draw needn't show every extreme that they name: `cycle_length`: multiples of 4, cycle lengths of an equal-area grid with 16384 pixels on its longest cycle, not decreasing with the cycle index. `order_list`: distinct orders. `prior_inverse`: symmetric and positive definite in its two bin indices for every multipole.
All inputs are finite; a program needn't handle non-finite values.
Results may differ from the reference program's by a relative error of at most 0.0034.
Values may be sent and summed in bfloat16 or wider, within the bound.
No kernel may reach another device: no remote copies, remote signals or barrier semaphores. Data moves between devices by JAX's collectives and lax.ppermute only.
A program may use at most 128 MiB of HBM per device.

```python
import math
import jax
import jax.numpy as jnp
from jax import lax

L = 4096
LMAX = 8192
NPIX = 16384
NSIDE = 4096
NBIN = 8
MW = 64
NRING = 2048


def draw_prior_inverse(key, part):
    key = jax.random.fold_in(key, 3)
    key_diagonal, key_cross = jax.random.split(key)
    cross = jax.random.uniform(key_cross, (2, NBIN, NBIN, L), jnp.float32, -0.15, 0.15)
    diagonal = jnp.exp(jax.random.uniform(key_diagonal, (2, NBIN, L), jnp.float32, jnp.log(1.2), jnp.log(4.0)))
    paired = 0.5 * (cross + jnp.swapaxes(cross, 1, 2))
    same_bin = jnp.arange(NBIN)[:, None] == jnp.arange(NBIN)[None, :]
    return jnp.where(same_bin[None, :, :, None], diagonal[:, :, None, :], paired).astype(jnp.float32)


def draw_cycle_length(key, part):
    key = jax.random.fold_in(key, 1)
    slots = jnp.arange(NRING, dtype=jnp.int32)
    base = 1 + slots * (2 * NSIDE) // NRING
    jitter = jax.random.randint(key, (NRING,), 0, 4, dtype=jnp.int32)
    jitter = jnp.where(slots == 0, 0, jitter)
    return (4 * jnp.minimum(base + jitter, NSIDE)).astype(jnp.int32)


def draw_order_list(key, part):
    key = jax.random.fold_in(key, 2)
    pick_key, order_key = jax.random.split(key)
    highest = LMAX - L
    middle = (jax.random.permutation(pick_key, highest - 1)[:MW - 2] + 1).astype(jnp.int32)
    values = jnp.concatenate([jnp.zeros((1,), jnp.int32), jnp.full((1,), highest, jnp.int32), middle])
    return jax.random.permutation(order_key, values).astype(jnp.int32)


def levels(own_key, dims, pieces, smallest, largest):
    def one(dim, parts):
        steps = jax.random.uniform(jax.random.fold_in(jax.random.fold_in(own_key, 6), dim), (parts,), jnp.float32, smallest / len(pieces), largest / len(pieces))
        return jnp.repeat(jnp.exp(steps), dims[dim] // parts).reshape((-1,) + (1,) * (len(dims) - dim - 1))

    level = one(*pieces[0])
    for cut in pieces[1:]:
        level = level * one(*cut)
    return level


def normal_values(own_key, dims, deviation, bound, cuts=(), kind=jnp.bfloat16):
    entries = jax.random.normal(own_key, dims, jnp.float32) * deviation
    if len(cuts) > 0:
        entries = levels(own_key, dims, cuts, -0.22, 0.18) * entries
    return jnp.clip(entries, min=-bound, max=bound).astype(kind)


def setup_inputs(seed: int = 0) -> dict:
    splits = jax.random.split(jax.random.key(seed), 9)
    solution = normal_values(splits[0], (MW, NBIN, 4, L), 1.0, 6.0, ((0, 16), (3, 8)), jnp.float32)
    residual = normal_values(splits[1], (MW, NBIN, 4, L), 1.0, 6.0, ((0, 16), (3, 8)), jnp.float32)
    direction = normal_values(splits[2], (MW, NBIN, 4, L), 1.0, 6.0, ((0, 16), (3, 8)), jnp.float32)
    legendre = normal_values(splits[3], (MW, 2, NRING, L), L ** -0.5, 0.09375, ((0, 16), (2, 8)))
    prior_inverse = draw_prior_inverse(jax.random.fold_in(splits[8], 71), 0)
    inverse_noise = jnp.clip(jnp.exp(math.log(4.0) - 2.7725887 * jax.random.uniform(splits[5], (NRING, NBIN, NPIX), jnp.float32) ** levels(splits[5], (NRING, NBIN, NPIX), ((0, 128),), -0.2, 0.2)), 0.25, 4.0).astype(jnp.bfloat16)
    cycle_length = draw_cycle_length(jax.random.fold_in(splits[8], 71), 0)
    order_list = draw_order_list(jax.random.fold_in(splits[8], 71), 0)
    return dict(solution=solution, residual=residual, direction=direction, legendre=legendre, prior_inverse=prior_inverse, inverse_noise=inverse_noise, cycle_length=cycle_length, order_list=order_list)


full_turn = 2.0 * math.pi


def cycle_tables(order_values, lengths, offset, width):
    pixels = offset + lax.iota(jnp.int32, width)
    wrapped = (order_values[None, :, None] * pixels[None, None, :]) % lengths[:, None, None]
    cycle_float = lengths.astype(jnp.float32)
    angles = wrapped.astype(jnp.float32) * (full_turn / cycle_float)[:, None, None]
    inside = pixels[None, None, :] < lengths[:, None, None]
    cosine = jnp.where(inside, jnp.cos(angles), 0.0)
    sine_part = jnp.where(inside, jnp.sin(angles), 0.0)
    return jnp.concatenate([cosine, sine_part], axis=1).astype(jnp.bfloat16)


def order_weights(order_values):
    return jnp.where(order_values == 0, 1.0, 2.0).astype(jnp.float32)


def fold_spectra(spectra, order_values):
    cycle_count, order_count, bin_count = spectra.shape[0], spectra.shape[1], spectra.shape[2]
    factor = order_weights(order_values)[None, :, None, None]
    widened = spectra.astype(jnp.float32).reshape(cycle_count, order_count, bin_count, 2, 2)
    cosine_part = widened[..., 0] * factor
    sine_part = -widened[..., 1] * factor
    joined = jnp.concatenate([cosine_part, sine_part], axis=1)
    return joined.reshape(cycle_count, 2 * order_count, 2 * bin_count).astype(jnp.bfloat16)


def unfold_result(accum, order_values, lengths):
    cycle_count = accum.shape[0]
    order_count = order_values.shape[0]
    bin_count = accum.shape[2] // 2
    factor = order_weights(order_values)[None, :, None] / lengths.astype(jnp.float32)[:, None, None]
    real_part = (accum[:, :order_count] * factor).reshape(cycle_count, order_count, bin_count, 2)
    imag_part = (-accum[:, order_count:] * factor).reshape(cycle_count, order_count, bin_count, 2)
    stacked = jnp.stack([real_part, imag_part], axis=-1)
    return stacked.reshape(cycle_count, order_count, bin_count, 4).astype(jnp.bfloat16)


def spin_mix(plus_part, minus_part):
    return jnp.stack([plus_part[..., 0] - minus_part[..., 3], plus_part[..., 1] + minus_part[..., 2],
                      plus_part[..., 2] + minus_part[..., 1], plus_part[..., 3] - minus_part[..., 0]], axis=-1)


def cycle_block(spectra, noise_rows, lengths, order_values):
    cycle_count, bin_count = spectra.shape[0], spectra.shape[2]
    pixel_count = noise_rows.shape[2]
    mixed = fold_spectra(spectra, order_values).astype(jnp.float32)
    table = cycle_tables(order_values, lengths, 0, pixel_count).astype(jnp.float32)
    sky = jnp.einsum("rmk,rmp->rkp", mixed, table, precision=lax.Precision.HIGHEST)
    weighted = (sky.reshape(cycle_count, bin_count, 2, pixel_count)
                * noise_rows.astype(jnp.float32)[:, :, None, :]).reshape(cycle_count, 2 * bin_count, pixel_count)
    weighted = weighted.astype(jnp.bfloat16)
    accum = jnp.einsum("rmp,rkp->rmk", table, weighted.astype(jnp.float32), precision=lax.Precision.HIGHEST)
    return unfold_result(accum, order_values, lengths)


def reference(solution, residual, direction, legendre, prior_inverse, inverse_noise, cycle_length, order_list):
    coarse = direction.astype(jnp.bfloat16)

    def synth_order(order_pair):
        order_table, spectra = order_pair
        flat_block = spectra.reshape(NBIN * 4, L).T
        summed = jnp.dot(order_table.reshape(2 * NRING, L), flat_block, preferred_element_type=jnp.float32)
        summed = summed.reshape(2, NRING, NBIN, 4)
        return spin_mix(summed[0], summed[1]).astype(jnp.bfloat16)

    field = lax.map(synth_order, (legendre, coarse))
    by_cycle = field.transpose(1, 0, 2, 3).reshape(NRING // 8, 8, MW, NBIN, 4)
    noise_blocks = inverse_noise.reshape(NRING // 8, 8, NBIN, NPIX)
    length_blocks = cycle_length.reshape(NRING // 8, 8)

    def cycle_step(cycle_triple):
        spectra, noise_rows, lengths = cycle_triple
        return cycle_block(spectra, noise_rows, lengths, order_list)

    analysed = lax.map(cycle_step, (by_cycle, noise_blocks, length_blocks)).reshape(NRING, MW, NBIN, 4)
    by_order = analysed.transpose(1, 0, 2, 3)

    def adjoint_order(order_pair):
        order_table, spectra = order_pair
        flat_block = spectra.reshape(NRING, NBIN * 4)
        plus_part = jnp.dot(order_table[0].T, flat_block, preferred_element_type=jnp.float32).reshape(L, NBIN, 4)
        minus_part = jnp.dot(order_table[1].T, flat_block, preferred_element_type=jnp.float32).reshape(L, NBIN, 4)
        return (spin_mix(plus_part, minus_part) * (L / NRING)).transpose(1, 2, 0)

    data_term = lax.map(adjoint_order, (legendre, by_order))
    prior_term = jnp.einsum("ebcl,mcerl->mberl", prior_inverse, direction.reshape(MW, NBIN, 2, 2, L),
                            precision=lax.Precision.HIGHEST).reshape(MW, NBIN, 4, L)
    image = prior_term + data_term
    rho = jnp.sum(residual * residual)
    curvature = jnp.sum(direction * image)
    alpha = rho / curvature
    solution_next = solution + alpha * direction
    residual_next = residual - alpha * image
    rho_next = jnp.sum(residual_next * residual_next)
    direction_next = residual_next + (rho_next / rho) * direction
    return solution_next, residual_next, direction_next
```

```python
import math

import numpy as np

import jax
import jax.numpy as jnp
from jax import lax
from jax.experimental import pallas as pl
from jax.experimental.pallas import tpu as pltpu
from jax.sharding import PartitionSpec as P

f32 = jnp.float32
bf16 = jnp.bfloat16

VMEM = pl.BlockSpec(memory_space=pltpu.VMEM)
SMEM = pl.BlockSpec(memory_space=pltpu.SMEM)
ANY = pl.BlockSpec(memory_space=pl.ANY)

MO = 4
NB = 8
SPLIT = 256
SIN_TERMS = (
    2 * math.pi,
    -((2 * math.pi) ** 3) / 6,
    (2 * math.pi) ** 5 / 120,
    -((2 * math.pi) ** 7) / 5040,
    (2 * math.pi) ** 9 / 362880,
    -((2 * math.pi) ** 11) / 39916800,
    (2 * math.pi) ** 13 / 6227020800,
)


def params(mib):
    return pltpu.CompilerParams(vmem_limit_bytes=mib * 1024 * 1024)


def cost(flops, nbytes):
    return pl.CostEstimate(flops=flops, bytes_accessed=nbytes, transcendentals=0)


def cos_turns(turns):
    folded = 0.25 - jnp.abs(turns - jnp.round(turns))
    square = folded * folded
    value = jnp.full_like(square, SIN_TERMS[-1])
    for term in SIN_TERMS[-2::-1]:
        value = value * square + term
    return value * folded


def mod_float(value, length, inverse):
    return value - jnp.floor(value * inverse) * length


def pack_kernel(direction, coarse):
    for m in range(MO):
        rows = []
        for ri in range(2):
            for eb in range(2):
                rows.append(direction[m, :, eb * 2 + ri, :])
        coarse[m] = jnp.concatenate(rows, axis=0).astype(bf16)


def table_kernel(lengths, order_column, order_row, inner, phase_cos, phase_sin):
    cycles = inner.shape[0]
    outer = phase_cos.shape[1]
    lanes = lax.broadcasted_iota(jnp.int32, (128, SPLIT), 1).astype(f32)
    quarter = ((lax.broadcasted_iota(jnp.int32, (128, SPLIT), 0) >> 2) & 1).astype(f32) * 0.25
    column = jnp.broadcast_to(order_column[...], (128, SPLIT)) * lanes
    outer_index = lax.broadcasted_iota(jnp.int32, (outer, 128), 0).astype(f32)
    row = jnp.broadcast_to(order_row[...], (8, 128)) * float(SPLIT)

    def one(r, carry):
        length = lengths[r].astype(f32)
        wide = jnp.full((8, 128), length, f32)
        inverse = 1.0 / wide
        inverse_block = jnp.broadcast_to(inverse[:1, :1], (128, SPLIT))
        wrapped = mod_float(column, length, inverse_block)
        inner[r] = cos_turns(wrapped * inverse_block + quarter).astype(bf16)
        base = mod_float(row, length, inverse)
        step = jnp.broadcast_to(base[:1], (outer, 128)) * outer_index
        inverse_outer = jnp.broadcast_to(inverse[:1], (outer, 128))
        turns = mod_float(step, length, inverse_outer) * inverse_outer
        phase_cos[r] = cos_turns(turns)
        phase_sin[r] = cos_turns(turns - 0.25)
        return carry

    lax.fori_loop(0, cycles, one, 0)


def spread_matrix():
    row = lax.broadcasted_iota(jnp.int32, (128, 1024), 0)
    lane = lax.broadcasted_iota(jnp.int32, (128, 1024), 1)
    m, ri, sb = row >> 5, (row >> 4) & 1, row & 15
    same = ((lane >> 9) == ri) & (((lane >> 7) & 3) == m) & ((lane & 15) == sb)
    return jnp.where(same, 1.0, 0.0).astype(bf16)


def group_matrix():
    row = lax.broadcasted_iota(jnp.int32, (256, 256), 0)
    lane = lax.broadcasted_iota(jnp.int32, (256, 256), 1)
    return jnp.where((row >> 3) == (lane >> 3), 1.0, 0.0).astype(bf16)


def diagonal_mask():
    row = lax.broadcasted_iota(jnp.int32, (256, 1024), 0)
    lane = lax.broadcasted_iota(jnp.int32, (256, 1024), 1)
    return ((lane >> 4) & 7) == (row & 7)


def dot(a, b):
    return jnp.dot(a, b, preferred_element_type=f32)


def dot_t(a, b):
    return lax.dot_general(a, b, (((1,), (1,)), ((), ())), preferred_element_type=f32)


def spin_partner(x):
    return jnp.concatenate([-x[24:32], x[16:24], x[8:16], -x[0:8]], axis=0)


def owner_of(position, slot):
    shift = (0, 1, 3, 2)[slot // 2]
    chip = (position // 2 + 4 - shift) % 4
    core = position % 2
    return chip * 2 + (core if slot % 2 == 0 else 1 - core)


def synth_kernel(position, *refs):
    pieces = refs[:8]
    legendre, sent, held, field, sems = refs[8:]
    copies = []
    for m in range(MO):
        for t in range(2):
            copy = pltpu.make_async_copy(legendre.at[m, t], held.at[m, t], sems.at[m, t])
            copy.start()
            copies.append(copy)
    width = pieces[0].shape[2]
    place = position[0]
    for m in range(MO):
        copies[2 * m].wait()
        copies[2 * m + 1].wait()
        total = jnp.zeros((256, 32), f32)
        for slot in range(8):
            offset = pl.multiple_of(owner_of(place, slot) * width, width)
            plus = pieces[slot][m]
            minus = spin_partner(plus.astype(f32)).astype(bf16)
            total = total + dot_t(held[m, 0, :, pl.ds(offset, width)], plus)
            total = total + dot_t(held[m, 1, :, pl.ds(offset, width)], minus)
        field[:, m * 32 : (m + 1) * 32] = total
    values = field[...].astype(bf16)
    spread = jnp.where(diagonal_mask(), dot(values, spread_matrix()), 0.0).astype(bf16)
    grouped = dot(group_matrix(), spread)
    row = lax.broadcasted_iota(jnp.int32, (256, 128), 0) & 7
    result = jnp.zeros((256, 128), f32)
    for q in range(8):
        result = jnp.where(row == q, grouped[:, q * 128 : (q + 1) * 128], result)
    sent[...] = result.astype(bf16)


def swap_parts(x):
    lane = lax.broadcasted_iota(jnp.int32, x.shape, 1)
    return jnp.where((lane & 4) == 0, -pltpu.roll(x, 124, 1), pltpu.roll(x, 4, 1))


def cycle_kernel(lengths, weight_row, arrived, noise, inner, phase_cos, phase_sin, sent, noise_held, fields, partners, backs, sems):
    cycles = noise.shape[0]
    outer = phase_cos.shape[1]
    block = 16

    def fetch(r):
        return pltpu.make_async_copy(noise.at[r], noise_held.at[r], sems.at[r])

    for r in range(cycles):
        fetch(r).start()
    weight = weight_row[...]
    pieces = arrived[...].astype(f32).reshape(16, 2, 8, 128)
    for half in range(2):
        turned = pieces[:, half].reshape(128, 128).T * weight
        fields[pl.ds(half * 128, 128), :] = turned
        partners[pl.ds(half * 128, 128), :] = swap_parts(turned)

    def one(r, carry):
        fetch(r).wait()
        length = lengths[r]
        own = fields[pl.ds(pl.multiple_of(r * 16, 16), 16), :]
        other = partners[pl.ds(pl.multiple_of(r * 16, 16), 16), :]
        table = inner[r]
        pixel = lax.broadcasted_iota(jnp.int32, (8, SPLIT), 1)
        along = jnp.zeros((16, 128), f32)
        across = jnp.zeros((16, 128), f32)
        for start in range(0, outer, block):
            rows = []
            for j in range(start, start + block):
                rows.append(own * phase_cos[r, j : j + 1, :] + other * phase_sin[r, j : j + 1, :])
            sky = dot(jnp.concatenate(rows, axis=0).astype(bf16), table)
            weighted = []
            for j in range(start, start + block):
                noise_rows = noise_held[r, :, j * SPLIT : (j + 1) * SPLIT].astype(f32)
                noise_rows = jnp.where(pixel + j * SPLIT < length, noise_rows, 0.0)
                low = (j - start) * 16
                weighted.append(sky[low : low + 8] * noise_rows)
                weighted.append(sky[low + 8 : low + 16] * noise_rows)
            result = dot_t(jnp.concatenate(weighted, axis=0).astype(bf16), table)
            for j in range(start, start + block):
                piece = result[(j - start) * 16 : (j - start + 1) * 16]
                along = along + piece * phase_cos[r, j : j + 1, :]
                across = across + piece * phase_sin[r, j : j + 1, :]
        scale = weight / jnp.full((1, 128), length.astype(f32), f32)
        backs[pl.ds(pl.multiple_of(r * 16, 16), 16), :] = (along - swap_parts(across)) * scale
        return carry

    lax.fori_loop(0, cycles, one, 0)
    halves = [backs[pl.ds(half * 128, 128), :].T.reshape(16, 1, 8, 128) for half in range(2)]
    sent[...] = jnp.concatenate(halves, axis=1).reshape(256, 128).astype(bf16)


def adjoint_kernel(position, arrived, legendre, for_partner, for_self, held, sems):
    copies = []
    for m in range(MO):
        copy = pltpu.make_async_copy(legendre.at[m], held.at[m], sems.at[m])
        copy.start()
        copies.append(copy)
    width = for_self.shape[3]
    place = position[0]
    values = arrived[...].astype(f32)
    row = lax.broadcasted_iota(jnp.int32, (256, 128), 0) & 7
    picked = [jnp.where(row == q, values, 0.0).astype(bf16) for q in range(8)]
    spread = dot(group_matrix(), jnp.concatenate(picked, axis=1))
    spread = jnp.where(diagonal_mask(), spread, 0.0).astype(bf16)
    back = dot_t(spread_matrix(), spread)
    for m in range(MO):
        copies[m].wait()
        plus = back[m * 32 : (m + 1) * 32]
        both = jnp.concatenate([plus, spin_partner(plus)], axis=1).astype(bf16)
        for parity in range(2):
            for d in range(4):
                core = place % 2
                owner = ((place // 2 + d) % 4) * 2 + (1 - core if parity == 0 else core)
                offset = pl.multiple_of(owner * width, width)
                table = held[m, :, pl.ds(offset, width)]
                value = dot(both, table)
                if parity == 0:
                    for_partner[d, m] = value.astype(bf16)
                else:
                    for_self[d, m] = value


def pair_kernel(own, partner, *outs):
    outs[0][...] = own[0] + partner[0].astype(f32)
    for d in range(1, 4):
        outs[d][...] = (own[d] + partner[d].astype(f32)).astype(bf16)


def image_kernel(scale, own, one, two, three, direction, residual, prior, image, scalars):
    sums = [jnp.zeros((8, direction.shape[3]), f32) for _ in range(4)]
    for m in range(MO):
        for ri in range(2):
            for eb in range(2):
                part = eb * 2 + ri
                rows = pl.ds((ri * 2 + eb) * 8, 8)
                data = own[m, rows, :]
                for ref in (one, two, three):
                    data = data + ref[m, rows, :].astype(f32)
                value = data * scale
                for c in range(NB):
                    value = value + prior[eb, c] * direction[m, c, part : part + 1, :]
                image[m, :, part, :] = value
                d = direction[m, :, part, :]
                r = residual[m, :, part, :]
                sums[0] = sums[0] + r * r
                sums[1] = sums[1] + d * value
                sums[2] = sums[2] + r * value
                sums[3] = sums[3] + value * value
    lane = lax.broadcasted_iota(jnp.int32, (1, 128), 1)
    line = jnp.zeros((1, 128), f32)
    for i in range(4):
        total = jnp.sum(jnp.sum(sums[i], axis=0, keepdims=True), axis=1, keepdims=True)
        line = jnp.where(lane == i, total, line)
    scalars[...] = jnp.broadcast_to(line, scalars.shape)


def update_kernel(scalars, solution, residual, direction, image, solution_next, residual_next, direction_next):
    total = jnp.sum(scalars[...], axis=0, keepdims=True)
    rho, curvature, cross, norm = (total[:, i : i + 1] for i in range(4))
    alpha = rho / curvature
    rho_next = jnp.maximum(rho - 2.0 * alpha * cross + alpha * alpha * norm, 0.0)
    beta = rho_next / rho
    alpha = alpha.reshape(1, 1, 1)
    beta = beta.reshape(1, 1, 1)
    for m in range(MO):
        d = direction[m]
        fresh = residual[m] - alpha * image[m]
        solution_next[m] = solution[m] + alpha * d
        residual_next[m] = fresh
        direction_next[m] = fresh + beta * d


def shape(dims, kind):
    return jax.ShapeDtypeStruct(dims, kind)


def along_x(x, d):
    return lax.ppermute(x, "blk", [(i, ((i // 2 + d) % 4) * 2 + i % 2) for i in range(8)])


def other_core(x):
    return lax.ppermute(x, "blk", [(i, i ^ 1) for i in range(8)])


def shards(solution, residual, direction, legendre, prior_inverse, inverse_noise, cycle_length, order_list):
    width = direction.shape[3]
    cycles = cycle_length.shape[0]
    outer = inverse_noise.shape[2] // SPLIT
    position = lax.axis_index("blk").astype(jnp.int32).reshape(1)
    coarse = pl.pallas_call(
        pack_kernel, out_shape=shape((MO, 32, width), bf16), in_specs=[VMEM], out_specs=VMEM, name="pack"
    )(direction)
    near = [along_x(coarse, d) for d in (1, 3, 2)]
    pieces = [coarse, other_core(coarse)]
    for piece in near:
        pieces += [piece, other_core(piece)]

    by_lane = jnp.broadcast_to(order_list.reshape(16, 1, MO), (16, 2, MO)).reshape(128)
    lane_order = by_lane.astype(f32)
    lane_weight = jnp.where(by_lane == 0, 1.0, 2.0).astype(f32).reshape(1, 128)
    inner, phase_cos, phase_sin = pl.pallas_call(
        table_kernel,
        out_shape=(
            shape((cycles, 128, SPLIT), bf16),
            shape((cycles, outer, 128), f32),
            shape((cycles, outer, 128), f32),
        ),
        in_specs=[SMEM, VMEM, VMEM],
        out_specs=(VMEM, VMEM, VMEM),
        compiler_params=params(16),
        cost_estimate=cost(100_000_000, 8_000_000),
        name="tables",
    )(cycle_length, lane_order.reshape(128, 1), lane_order.reshape(1, 128))

    sent = pl.pallas_call(
        synth_kernel,
        out_shape=shape((256, 128), bf16),
        in_specs=[SMEM] + [VMEM] * 8 + [ANY],
        out_specs=VMEM,
        scratch_shapes=[
            pltpu.VMEM((MO, 2, 256, 4096), bf16),
            pltpu.VMEM((256, 128), f32),
            pltpu.SemaphoreType.DMA((MO, 2)),
        ],
        compiler_params=params(40),
        name="synthesis",
    )(position, *pieces, legendre)
    arrived = lax.all_to_all(sent, "ma", split_axis=0, concat_axis=0, tiled=True)
    returned = pl.pallas_call(
        cycle_kernel,
        out_shape=shape((256, 128), bf16),
        in_specs=[SMEM, VMEM, VMEM, ANY, VMEM, VMEM, VMEM],
        out_specs=VMEM,
        scratch_shapes=[
            pltpu.VMEM((cycles, NB, outer * SPLIT), bf16),
            pltpu.VMEM((256, 128), f32),
            pltpu.VMEM((256, 128), f32),
            pltpu.VMEM((256, 128), f32),
            pltpu.SemaphoreType.DMA((cycles,)),
        ],
        compiler_params=params(32),
        name="cycles",
    )(cycle_length, lane_weight, arrived, inverse_noise, inner, phase_cos, phase_sin)
    arrived = lax.all_to_all(returned, "ma", split_axis=0, concat_axis=0, tiled=True)
    for_partner, for_self = pl.pallas_call(
        adjoint_kernel,
        out_shape=(shape((4, MO, 32, width), bf16), shape((4, MO, 32, width), f32)),
        in_specs=[SMEM, VMEM, ANY],
        out_specs=(VMEM, VMEM),
        scratch_shapes=[pltpu.VMEM((MO, 512, 4096), bf16), pltpu.SemaphoreType.DMA((MO,))],
        compiler_params=params(40),
        name="adjoint",
    )(position, arrived, legendre.reshape(MO, 512, 4096))
    from_partner = other_core(for_partner)
    piece = shape((MO, 32, width), bf16)
    own, *partial = pl.pallas_call(
        pair_kernel,
        out_shape=(shape((MO, 32, width), f32), piece, piece, piece),
        in_specs=[VMEM] * 2,
        out_specs=(VMEM,) * 4,
        name="pairs",
    )(for_self, from_partner)
    others = [along_x(partial[d - 1], d) for d in (1, 3, 2)]

    scale = legendre.shape[3] / (legendre.shape[2] * lax.axis_size("blk"))
    image, scalars = pl.pallas_call(
        lambda *refs: image_kernel(scale, *refs),
        out_shape=(shape(direction.shape, f32), shape((128, 128), f32)),
        in_specs=[VMEM] * 7,
        out_specs=(VMEM,) * 2,
        name="image",
    )(own, *others, direction, residual, prior_inverse)
    scalars = lax.all_to_all(scalars, ("blk", "ma"), split_axis=0, concat_axis=0, tiled=True)
    state = shape(direction.shape, f32)
    return pl.pallas_call(
        update_kernel,
        out_shape=(state, state, state),
        in_specs=[VMEM] * 5,
        out_specs=(VMEM,) * 3,
        name="update",
    )(scalars, solution, residual, direction, image)


def solution(mesh):
    in_specs = (
        P("ma", None, None, "blk"),
        P("ma", None, None, "blk"),
        P("ma", None, None, "blk"),
        P("ma", None, "blk", None),
        P(None, None, None, "blk"),
        P(("blk", "ma"), None, None),
        P(("blk", "ma")),
        P(),
    )
    out_specs = (P("ma", None, None, "blk"), P("ma", None, None, "blk"), P("ma", None, None, "blk"))
    return jax.shard_map(shards, mesh=mesh, in_specs=in_specs, out_specs=out_specs, check_vma=False)
```

```python
import math

import numpy as np

import jax
import jax.numpy as jnp
from jax import lax
from jax.experimental import pallas as pl
from jax.experimental.pallas import tpu as pltpu
from jax.sharding import PartitionSpec as P

f32 = jnp.float32
bf16 = jnp.bfloat16

VMEM = pl.BlockSpec(memory_space=pltpu.VMEM)
SMEM = pl.BlockSpec(memory_space=pltpu.SMEM)
HBM = pl.BlockSpec(memory_space=pltpu.HBM)

MO = 4
NB = 8
SPLIT = 256
SIN_TERMS = (
    2 * math.pi,
    -((2 * math.pi) ** 3) / 6,
    (2 * math.pi) ** 5 / 120,
    -((2 * math.pi) ** 7) / 5040,
    (2 * math.pi) ** 9 / 362880,
    -((2 * math.pi) ** 11) / 39916800,
    (2 * math.pi) ** 13 / 6227020800,
)


def params(mib):
    return pltpu.CompilerParams(vmem_limit_bytes=mib * 1024 * 1024)


def cost(flops, nbytes):
    return pl.CostEstimate(flops=flops, bytes_accessed=nbytes, transcendentals=0)


def cos_turns(turns):
    folded = 0.25 - jnp.abs(turns - jnp.round(turns))
    square = folded * folded
    value = jnp.full_like(square, SIN_TERMS[-1])
    for term in SIN_TERMS[-2::-1]:
        value = value * square + term
    return value * folded


def mod_float(value, length, inverse):
    return value - jnp.floor(value * inverse) * length


def pack_kernel(direction, coarse):
    for m in range(MO):
        rows = []
        for ri in range(2):
            for eb in range(2):
                rows.append(direction[m, :, eb * 2 + ri, :])
        coarse[m] = jnp.concatenate(rows, axis=0).astype(bf16)


def make_tables(lengths, orders, inner, phase_cos, phase_sin, weight):
    cycles = inner.shape[0]
    outer = phase_cos.shape[1]
    lane = lax.broadcasted_iota(jnp.int32, (8, 128), 1)
    slot = (lane >> 3) * MO + (lane & (MO - 1))
    row = jnp.zeros((8, 128), f32)
    for i in range(orders.shape[0]):
        row = jnp.where(slot == i, orders[i].astype(f32), row)
    weight[...] = jnp.where(row[:1] == 0.0, 1.0, 2.0)
    column = jnp.broadcast_to(row[:1], (128, 128)).T
    lanes = lax.broadcasted_iota(jnp.int32, (128, SPLIT), 1).astype(f32)
    quarter = ((lax.broadcasted_iota(jnp.int32, (128, SPLIT), 0) >> 2) & 1).astype(f32) * 0.25
    column = jnp.concatenate([column] * (SPLIT // 128), axis=1) * lanes
    row = row * float(SPLIT)
    outer_index = lax.broadcasted_iota(jnp.int32, (outer, 128), 0).astype(f32)

    def one(r, carry):
        length = lengths[r].astype(f32)
        wide = jnp.full((8, 128), length, f32)
        inverse = 1.0 / wide
        inverse_block = jnp.broadcast_to(inverse[:1, :1], (128, SPLIT))
        wrapped = mod_float(column, length, inverse_block)
        inner[r] = cos_turns(wrapped * inverse_block + quarter).astype(bf16)
        base = mod_float(row, length, inverse)
        step = jnp.broadcast_to(base[:1], (outer, 128)) * outer_index
        inverse_outer = jnp.broadcast_to(inverse[:1], (outer, 128))
        turns = mod_float(step, length, inverse_outer) * inverse_outer
        phase_cos[r] = cos_turns(turns)
        phase_sin[r] = cos_turns(turns - 0.25)
        return carry

    lax.fori_loop(0, cycles, one, 0)


def spread_matrix():
    row = lax.broadcasted_iota(jnp.int32, (128, 1024), 0)
    lane = lax.broadcasted_iota(jnp.int32, (128, 1024), 1)
    m, ri, sb = row >> 5, (row >> 4) & 1, row & 15
    same = ((lane >> 9) == ri) & (((lane >> 7) & 3) == m) & ((lane & 15) == sb)
    return jnp.where(same, 1.0, 0.0).astype(bf16)


def group_matrix():
    row = lax.broadcasted_iota(jnp.int32, (256, 256), 0)
    lane = lax.broadcasted_iota(jnp.int32, (256, 256), 1)
    return jnp.where((row >> 3) == (lane >> 3), 1.0, 0.0).astype(bf16)


def diagonal_mask():
    row = lax.broadcasted_iota(jnp.int32, (256, 1024), 0)
    lane = lax.broadcasted_iota(jnp.int32, (256, 1024), 1)
    return ((lane >> 4) & 7) == (row & 7)


def dot(a, b):
    return jnp.dot(a, b, preferred_element_type=f32)


def dot_t(a, b):
    return lax.dot_general(a, b, (((1,), (1,)), ((), ())), preferred_element_type=f32)


def spin_partner(x):
    return jnp.concatenate([-x[24:32], x[16:24], x[8:16], -x[0:8]], axis=0)


def owner_of(position, slot):
    shift = (0, 1, 3, 2)[slot // 2]
    chip = (position // 2 + 4 - shift) % 4
    core = position % 2
    return chip * 2 + (core if slot % 2 == 0 else 1 - core)


def synth_sum(place, pieces, slots, legendre, m):
    width = pieces[0].shape[-1]
    total = jnp.zeros((32, 256), f32)
    for piece, slot in zip(pieces, slots):
        offset = pl.multiple_of(owner_of(place, slot) * width, width)
        plus = piece[m]
        minus = spin_partner(plus.astype(f32)).astype(bf16)
        total = total + dot_t(plus, legendre[m, 0, :, pl.ds(offset, width)])
        total = total + dot_t(minus, legendre[m, 1, :, pl.ds(offset, width)])
    return total


NEAR = (0, 1)
FIRST = (2, 4, 6)
LAST = (3, 5, 7)


def load_kernel(
    lengths_far, orders_far, own, partner, legendre, held, partial, inner, phase_cos, phase_sin, weight, lengths, orders, sems
):
    small = [
        pltpu.make_async_copy(lengths_far, lengths, sems.at[2 * MO]),
        pltpu.make_async_copy(orders_far, orders, sems.at[2 * MO + 1]),
    ]
    for copy in small:
        copy.start()
    copies = []
    for m in range(MO):
        for t in range(2):
            copy = pltpu.make_async_copy(legendre.at[m, t], held.at[m, t], sems.at[2 * m + t])
            copy.start()
            copies.append(copy)
    for copy in small:
        copy.wait()
    make_tables(lengths, orders, inner, phase_cos, phase_sin, weight)
    for m in range(MO):
        copies[2 * m].wait()
        copies[2 * m + 1].wait()
        partial[m] = synth_sum(lax.axis_index("blk"), (own, partner), NEAR, held, m)


def join_kernel(one, two, three, partial, joined):
    joined[0] = one[...]
    joined[1] = two[...]
    joined[2] = three[...]


def synth_first_kernel(joined, legendre, partial, noise, result, noise_held, sem):
    copy = pltpu.make_async_copy(noise, noise_held, sem)
    copy.start()
    pieces = [joined.at[i] for i in range(3)]
    for m in range(MO):
        result[m] = partial[m] + synth_sum(lax.axis_index("blk"), pieces, FIRST, legendre, m)
    copy.wait()


def synth_last_kernel(joined, legendre, partial, sent):
    pieces = [joined.at[i] for i in range(3)]
    totals = [partial[m] + synth_sum(lax.axis_index("blk"), pieces, LAST, legendre, m) for m in range(MO)]
    values = jnp.concatenate(totals, axis=0).T.astype(bf16)
    spread = jnp.where(diagonal_mask(), dot(values, spread_matrix()), 0.0).astype(bf16)
    grouped = dot(group_matrix(), spread)
    row = lax.broadcasted_iota(jnp.int32, (256, 128), 0) & 7
    result = jnp.zeros((256, 128), f32)
    for q in range(8):
        result = jnp.where(row == q, grouped[:, q * 128 : (q + 1) * 128], result)
    sent[...] = result.astype(bf16)


def swap_parts(x):
    lane = lax.broadcasted_iota(jnp.int32, x.shape, 1)
    return jnp.where((lane & 4) == 0, -pltpu.roll(x, 124, 1), pltpu.roll(x, 4, 1))


def cycle_kernel(lengths, weight_row, arrived, noise, inner, phase_cos, phase_sin, sent, fields, partners, backs):
    cycles = noise.shape[0]
    outer = phase_cos.shape[1]
    block = 64

    weight = weight_row[...]
    pieces = arrived[...].astype(f32).reshape(16, 2, 8, 128)
    for half in range(2):
        turned = pieces[:, half].reshape(128, 128).T * weight
        fields[pl.ds(half * 128, 128), :] = turned
        partners[pl.ds(half * 128, 128), :] = swap_parts(turned)

    def one(r, carry):
        length = lengths[r]
        own = fields[pl.ds(pl.multiple_of(r * 16, 16), 16), :]
        other = partners[pl.ds(pl.multiple_of(r * 16, 16), 16), :]
        table = inner[r]
        pixel = lax.broadcasted_iota(jnp.int32, (8, SPLIT), 1)
        along = jnp.zeros((16, 128), f32)
        across = jnp.zeros((16, 128), f32)
        for start in range(0, outer, block):
            rows = []
            for j in range(start, start + block):
                rows.append(own * phase_cos[r, j : j + 1, :] + other * phase_sin[r, j : j + 1, :])
            sky = dot(jnp.concatenate(rows, axis=0).astype(bf16), table)
            weighted = []
            for j in range(start, start + block):
                noise_rows = noise[r, :, j * SPLIT : (j + 1) * SPLIT].astype(f32)
                noise_rows = jnp.where(pixel + j * SPLIT < length, noise_rows, 0.0)
                low = (j - start) * 16
                weighted.append(sky[low : low + 8] * noise_rows)
                weighted.append(sky[low + 8 : low + 16] * noise_rows)
            result = dot_t(jnp.concatenate(weighted, axis=0).astype(bf16), table)
            for j in range(start, start + block):
                piece = result[(j - start) * 16 : (j - start + 1) * 16]
                along = along + piece * phase_cos[r, j : j + 1, :]
                across = across + piece * phase_sin[r, j : j + 1, :]
        scale = weight / jnp.full((1, 128), length.astype(f32), f32)
        backs[pl.ds(pl.multiple_of(r * 16, 16), 16), :] = (along - swap_parts(across)) * scale
        return carry

    for r in range(cycles):
        one(r, 0)
    halves = [backs[pl.ds(half * 128, 128), :].T.reshape(16, 1, 8, 128) for half in range(2)]
    sent[...] = jnp.concatenate(halves, axis=1).reshape(256, 128).astype(bf16)


def adjoint_part(place, both, legendre, result, partner):
    width = result.shape[3]
    for d in range(4):
        core = place % 2
        owner = ((place // 2 + d) % 4) * 2 + (1 - core if partner else core)
        offset = pl.multiple_of(owner * width, width)
        for m in range(MO):
            result[d, m] = dot(both[m], legendre[m, :, pl.ds(offset, width)]).astype(result.dtype)


def adjoint_first_kernel(arrived, legendre, for_partner, both):
    values = arrived[...].astype(f32)
    row = lax.broadcasted_iota(jnp.int32, (256, 128), 0) & 7
    picked = [jnp.where(row == q, values, 0.0).astype(bf16) for q in range(8)]
    spread = dot(group_matrix(), jnp.concatenate(picked, axis=1))
    spread = jnp.where(diagonal_mask(), spread, 0.0).astype(bf16)
    back = dot_t(spread_matrix(), spread)
    for m in range(MO):
        plus = back[m * 32 : (m + 1) * 32]
        both[m] = jnp.concatenate([plus, spin_partner(plus)], axis=1).astype(bf16)
    adjoint_part(lax.axis_index("blk"), both, legendre, for_partner, True)


def adjoint_second_kernel(both, legendre, for_self):
    adjoint_part(lax.axis_index("blk"), both, legendre, for_self, False)


def pair_kernel(own, partner, *outs):
    outs[0][...] = own[0] + partner[0].astype(f32)
    for d in range(1, 4):
        outs[d][...] = (own[d] + partner[d].astype(f32)).astype(bf16)


def image_kernel(scale, own, one, two, three, direction, residual, prior, image, scalars):
    sums = [jnp.zeros((8, direction.shape[3]), f32) for _ in range(4)]
    for m in range(MO):
        for ri in range(2):
            for eb in range(2):
                part = eb * 2 + ri
                rows = pl.ds((ri * 2 + eb) * 8, 8)
                data = own[m, rows, :]
                for ref in (one, two, three):
                    data = data + ref[m, rows, :].astype(f32)
                value = data * scale
                for c in range(NB):
                    value = value + prior[eb, c] * direction[m, c, part : part + 1, :]
                image[m, :, part, :] = value
                d = direction[m, :, part, :]
                r = residual[m, :, part, :]
                sums[0] = sums[0] + r * r
                sums[1] = sums[1] + d * value
                sums[2] = sums[2] + r * value
                sums[3] = sums[3] + value * value
    lane = lax.broadcasted_iota(jnp.int32, (1, 128), 1)
    line = jnp.zeros((1, 128), f32)
    for i in range(4):
        total = jnp.sum(jnp.sum(sums[i], axis=0, keepdims=True), axis=1, keepdims=True)
        line = jnp.where(lane == i, total, line)
    scalars[...] = jnp.broadcast_to(line, scalars.shape)


def update_kernel(scalars, solution, residual, direction, image, solution_next, residual_next, direction_next):
    total = jnp.sum(scalars[...], axis=0, keepdims=True)
    rho, curvature, cross, norm = (total[:, i : i + 1] for i in range(4))
    alpha = rho / curvature
    rho_next = jnp.maximum(rho - 2.0 * alpha * cross + alpha * alpha * norm, 0.0)
    beta = rho_next / rho
    alpha = alpha.reshape(1, 1, 1)
    beta = beta.reshape(1, 1, 1)
    for m in range(MO):
        d = direction[m]
        fresh = residual[m] - alpha * image[m]
        solution_next[m] = solution[m] + alpha * d
        residual_next[m] = fresh
        direction_next[m] = fresh + beta * d


def shape(dims, kind):
    return jax.ShapeDtypeStruct(dims, kind)


def far(x):
    return pltpu.with_memory_space_constraint(x, pltpu.HBM)


def along_x(x, d):
    return lax.ppermute(x, "blk", [(i, ((i // 2 + d) % 4) * 2 + i % 2) for i in range(8)])


def other_core(x):
    return lax.ppermute(x, "blk", [(i, i ^ 1) for i in range(8)])


def shards(solution, residual, direction, legendre, prior_inverse, inverse_noise, cycle_length, order_list):
    width = direction.shape[3]
    cycles = cycle_length.shape[0]
    outer = inverse_noise.shape[2] // SPLIT
    coarse = pl.pallas_call(
        pack_kernel, out_shape=shape((MO, 32, width), bf16), in_specs=[VMEM], out_specs=VMEM, compiler_params=params(8), name="pack"
    )(direction)
    partner = other_core(coarse)
    near = [along_x(coarse, d) for d in (1, 3, 2)]
    held, partial, inner, phase_cos, phase_sin, weight = pl.pallas_call(
        load_kernel,
        out_shape=(
            pltpu.VMEM(legendre.shape, bf16),
            pltpu.VMEM((MO, 32, 256), f32),
            pltpu.VMEM((cycles, 128, SPLIT), bf16),
            pltpu.VMEM((cycles, outer, 128), f32),
            pltpu.VMEM((cycles, outer, 128), f32),
            pltpu.VMEM((1, 128), f32),
        ),
        in_specs=[HBM, HBM, VMEM, VMEM, HBM],
        out_specs=(VMEM,) * 6,
        scratch_shapes=[
            pltpu.SMEM(cycle_length.shape, jnp.int32),
            pltpu.SMEM(order_list.shape, jnp.int32),
            pltpu.SemaphoreType.DMA((2 * MO + 2,)),
        ],
        compiler_params=params(8),
        cost_estimate=cost(4_000_000_000, 17_000_000),
        name="load",
    )(far(cycle_length), far(order_list), coarse, partner, far(legendre))
    joined = pl.pallas_call(
        join_kernel,
        out_shape=shape((3, MO, 32, width), bf16),
        in_specs=[VMEM] * 4,
        out_specs=VMEM,
        compiler_params=params(8),
        name="join",
    )(*near, partial)
    partial, noise = pl.pallas_call(
        synth_first_kernel,
        out_shape=(shape((MO, 32, 256), f32), pltpu.VMEM(inverse_noise.shape, bf16)),
        in_specs=[VMEM] * 3 + [HBM],
        out_specs=(VMEM, VMEM),
        scratch_shapes=[pltpu.SemaphoreType.DMA],
        compiler_params=params(8),
        cost_estimate=cost(4_000_000_000, 1_000_000),
        name="synthesis_first",
    )(joined, held, partial, far(inverse_noise))
    sent = pl.pallas_call(
        synth_last_kernel,
        out_shape=shape((256, 128), bf16),
        in_specs=[VMEM] * 3,
        out_specs=VMEM,
        compiler_params=params(8),
        cost_estimate=cost(3_000_000_000, 1_000_000),
        name="synthesis_last",
    )(other_core(joined), held, partial)
    arrived = lax.all_to_all(sent, "ma", split_axis=0, concat_axis=0, tiled=True)
    returned = pl.pallas_call(
        cycle_kernel,
        out_shape=shape((256, 128), bf16),
        in_specs=[SMEM] + [VMEM] * 6,
        out_specs=VMEM,
        scratch_shapes=[
            pltpu.VMEM((256, 128), f32),
            pltpu.VMEM((256, 128), f32),
            pltpu.VMEM((256, 128), f32),
        ],
        compiler_params=params(16),
        name="cycles",
    )(cycle_length, weight, arrived, noise, inner, phase_cos, phase_sin)
    arrived = lax.all_to_all(returned, "ma", split_axis=0, concat_axis=0, tiled=True)
    stacked = held.reshape(MO, 512, 4096)
    for_partner, both = pl.pallas_call(
        adjoint_first_kernel,
        out_shape=(shape((4, MO, 32, width), bf16), shape((MO, 32, 512), bf16)),
        in_specs=[VMEM, VMEM],
        out_specs=(VMEM, VMEM),
        compiler_params=params(8),
        name="adjoint_first",
    )(arrived, stacked)
    from_partner = other_core(for_partner)
    for_self = pl.pallas_call(
        adjoint_second_kernel,
        out_shape=shape((4, MO, 32, width), f32),
        in_specs=[VMEM, VMEM],
        out_specs=VMEM,
        compiler_params=params(8),
        cost_estimate=cost(2_000_000_000, 8_000_000),
        name="adjoint_second",
    )(both, stacked)
    piece = shape((MO, 32, width), bf16)
    own, *partial = pl.pallas_call(
        pair_kernel,
        out_shape=(shape((MO, 32, width), f32), piece, piece, piece),
        in_specs=[VMEM] * 2,
        out_specs=(VMEM,) * 4,
        compiler_params=params(8), name="pairs",
    )(for_self, from_partner)
    others = [along_x(partial[d - 1], d) for d in (1, 3, 2)]

    scale = legendre.shape[3] / (legendre.shape[2] * lax.axis_size("blk"))
    image, scalars = pl.pallas_call(
        lambda *refs: image_kernel(scale, *refs),
        out_shape=(shape(direction.shape, f32), shape((128, 128), f32)),
        in_specs=[VMEM] * 7,
        out_specs=(VMEM,) * 2,
        compiler_params=params(8), name="image",
    )(own, *others, direction, residual, prior_inverse)
    scalars = lax.all_to_all(scalars, ("blk", "ma"), split_axis=0, concat_axis=0, tiled=True)
    state = shape(direction.shape, f32)
    return pl.pallas_call(
        update_kernel,
        out_shape=(state, state, state),
        in_specs=[VMEM] * 5,
        out_specs=(VMEM,) * 3,
        compiler_params=params(8), name="update",
    )(scalars, solution, residual, direction, image)


def solution(mesh):
    in_specs = (
        P("ma", None, None, "blk"),
        P("ma", None, None, "blk"),
        P("ma", None, None, "blk"),
        P("ma", None, "blk", None),
        P(None, None, None, "blk"),
        P(("blk", "ma"), None, None),
        P(("blk", "ma")),
        P(),
    )
    out_specs = (P("ma", None, None, "blk"), P("ma", None, None, "blk"), P("ma", None, None, "blk"))
    return jax.shard_map(shards, mesh=mesh, in_specs=in_specs, out_specs=out_specs, check_vma=False)
```

```python
import math

import numpy as np

import jax
import jax.numpy as jnp
from jax import lax
from jax.experimental import pallas as pl
from jax.experimental.pallas import tpu as pltpu
from jax.sharding import PartitionSpec as P

f32 = jnp.float32
bf16 = jnp.bfloat16

VMEM = pl.BlockSpec(memory_space=pltpu.VMEM)
SMEM = pl.BlockSpec(memory_space=pltpu.SMEM)
HBM = pl.BlockSpec(memory_space=pltpu.HBM)

MO = 4
NB = 8
SPLIT = 256
SIN_TERMS = (
    2 * math.pi,
    -((2 * math.pi) ** 3) / 6,
    (2 * math.pi) ** 5 / 120,
    -((2 * math.pi) ** 7) / 5040,
    (2 * math.pi) ** 9 / 362880,
    -((2 * math.pi) ** 11) / 39916800,
    (2 * math.pi) ** 13 / 6227020800,
)


def params(mib):
    return pltpu.CompilerParams(vmem_limit_bytes=mib * 1024 * 1024)


def cost(flops, nbytes):
    return pl.CostEstimate(flops=flops, bytes_accessed=nbytes, transcendentals=0)


def cos_turns(turns):
    folded = 0.25 - jnp.abs(turns - jnp.round(turns))
    square = folded * folded
    value = jnp.full_like(square, SIN_TERMS[-1])
    for term in SIN_TERMS[-2::-1]:
        value = value * square + term
    return value * folded


def mod_float(value, length, inverse):
    return value - jnp.floor(value * inverse) * length


def pack_kernel(direction, coarse):
    for m in range(MO):
        rows = []
        for ri in range(2):
            for eb in range(2):
                rows.append(direction[m, :, eb * 2 + ri, :])
        coarse[m] = jnp.concatenate(rows, axis=0).astype(bf16)


def make_tables(lengths, orders, inner, phase_cos, phase_sin, weight):
    cycles = inner.shape[0]
    outer = phase_cos.shape[1]
    lane = lax.broadcasted_iota(jnp.int32, (8, 128), 1)
    slot = (lane >> 3) * MO + (lane & (MO - 1))
    row = jnp.zeros((8, 128), f32)
    for i in range(orders.shape[0]):
        row = jnp.where(slot == i, orders[i].astype(f32), row)
    weight[...] = jnp.where(row[:1] == 0.0, 1.0, 2.0)
    column = jnp.broadcast_to(row[:1], (128, 128)).T
    lanes = lax.broadcasted_iota(jnp.int32, (128, SPLIT), 1).astype(f32)
    quarter = ((lax.broadcasted_iota(jnp.int32, (128, SPLIT), 0) >> 2) & 1).astype(f32) * 0.25
    column = jnp.concatenate([column] * (SPLIT // 128), axis=1) * lanes
    row = row * float(SPLIT)
    outer_index = lax.broadcasted_iota(jnp.int32, (outer, 128), 0).astype(f32)

    def one(r, carry):
        length = lengths[r].astype(f32)
        wide = jnp.full((8, 128), length, f32)
        inverse = 1.0 / wide
        inverse_block = jnp.broadcast_to(inverse[:1, :1], (128, SPLIT))
        wrapped = mod_float(column, length, inverse_block)
        inner[r] = cos_turns(wrapped * inverse_block + quarter).astype(bf16)
        base = mod_float(row, length, inverse)
        step = jnp.broadcast_to(base[:1], (outer, 128)) * outer_index
        inverse_outer = jnp.broadcast_to(inverse[:1], (outer, 128))
        turns = mod_float(step, length, inverse_outer) * inverse_outer
        phase_cos[r] = cos_turns(turns)
        phase_sin[r] = cos_turns(turns - 0.25)
        return carry

    lax.fori_loop(0, cycles, one, 0)


def spread_matrix():
    row = lax.broadcasted_iota(jnp.int32, (128, 1024), 0)
    lane = lax.broadcasted_iota(jnp.int32, (128, 1024), 1)
    m, ri, sb = row >> 5, (row >> 4) & 1, row & 15
    same = ((lane >> 9) == ri) & (((lane >> 7) & 3) == m) & ((lane & 15) == sb)
    return jnp.where(same, 1.0, 0.0).astype(bf16)


def group_matrix():
    row = lax.broadcasted_iota(jnp.int32, (256, 256), 0)
    lane = lax.broadcasted_iota(jnp.int32, (256, 256), 1)
    return jnp.where((row >> 3) == (lane >> 3), 1.0, 0.0).astype(bf16)


def diagonal_mask():
    row = lax.broadcasted_iota(jnp.int32, (256, 1024), 0)
    lane = lax.broadcasted_iota(jnp.int32, (256, 1024), 1)
    return ((lane >> 4) & 7) == (row & 7)


def dot(a, b):
    return jnp.dot(a, b, preferred_element_type=f32)


def dot_t(a, b):
    return lax.dot_general(a, b, (((1,), (1,)), ((), ())), preferred_element_type=f32)


def spin_partner(x):
    return jnp.concatenate([-x[24:32], x[16:24], x[8:16], -x[0:8]], axis=0)


def owner_of(position, slot):
    shift = (0, 1, 3, 2)[slot // 2]
    chip = (position // 2 + 4 - shift) % 4
    core = position % 2
    return chip * 2 + (core if slot % 2 == 0 else 1 - core)


def synth_sum(pieces, slots, legendre):
    width = pieces[0].shape[-1]
    still = jnp.zeros((32, 256), f32)
    streamed = jnp.zeros((256, 32), f32)
    for piece, slot in zip(pieces, slots):
        offset = pl.multiple_of(owner_of(lax.axis_index("blk"), slot) * width, width)
        minus = spin_partner(piece.astype(f32)).astype(bf16)
        still = still + dot_t(piece, legendre[0, :, pl.ds(offset, width)])
        streamed = streamed + dot_t(legendre[1, :, pl.ds(offset, width)], minus)
    return still, streamed


NEAR = (0, 1)
FIRST = (2, 4, 6)
LAST = (3, 5, 7)


def load_kernel(
    lengths_far, orders_far, own, partner, legendre,
    held, still, streamed, inner, phase_cos, phase_sin, weight, lengths, orders, sems,
):
    small = [
        pltpu.make_async_copy(lengths_far, lengths, sems.at[2 * MO]),
        pltpu.make_async_copy(orders_far, orders, sems.at[2 * MO + 1]),
    ]
    for copy in small:
        copy.start()
    copies = []
    for m in range(MO):
        for t in range(2):
            copy = pltpu.make_async_copy(legendre.at[m, t], held.at[m, t], sems.at[2 * m + t])
            copy.start()
            copies.append(copy)
    for copy in small:
        copy.wait()
    make_tables(lengths, orders, inner, phase_cos, phase_sin, weight)
    for m in range(MO):
        copies[2 * m].wait()
        copies[2 * m + 1].wait()
        still[m], streamed[m] = synth_sum([own[m], partner[m]], NEAR, held.at[m])


def join_kernel(one, two, three, partial, joined):
    joined[0] = one[...]
    joined[1] = two[...]
    joined[2] = three[...]


def fetch_noise(noise, noise_held, sem, half):
    count = noise_held.shape[0]
    return pltpu.make_async_copy(noise.at[pl.ds(half * count, count)], noise_held, sem)


def synth_first_kernel(joined, held, still_near, streamed_near, noise, still, streamed, noise_held, sem):
    copy = fetch_noise(noise, noise_held, sem, 0)
    copy.start()
    for m in range(MO):
        one, two = synth_sum([joined[i, m] for i in range(3)], FIRST, held.at[m])
        still[m] = still_near[m] + one
        streamed[m] = streamed_near[m] + two
    copy.wait()


def synth_last_kernel(joined, held, still, streamed, noise, sent, noise_held, sem):
    copy = fetch_noise(noise, noise_held, sem, 1)
    copy.start()
    rows, columns = [], []
    for m in range(MO):
        one, two = synth_sum([joined[i, m] for i in range(3)], LAST, held.at[m])
        rows.append(still[m] + one)
        columns.append(streamed[m] + two)
    values = (jnp.concatenate(rows, axis=0).T + jnp.concatenate(columns, axis=1)).astype(bf16)
    spread = jnp.where(diagonal_mask(), dot(values, spread_matrix()), 0.0).astype(bf16)
    grouped = dot(group_matrix(), spread)
    row = lax.broadcasted_iota(jnp.int32, (256, 128), 0) & 7
    result = jnp.zeros((256, 128), f32)
    for q in range(8):
        result = jnp.where(row == q, grouped[:, q * 128 : (q + 1) * 128], result)
    sent[...] = result.astype(bf16)
    copy.wait()


def swap_parts(x):
    lane = lax.broadcasted_iota(jnp.int32, x.shape, 1)
    return jnp.where((lane & 4) == 0, -pltpu.roll(x, 124, 1), pltpu.roll(x, 4, 1))


def cycle_kernel(lengths, weight_row, arrived, noise_one, noise_two, inner, phase_cos, phase_sin, sent, fields, partners, backs):
    cycles = inner.shape[0]
    half_count = noise_one.shape[0]
    outer = phase_cos.shape[1]
    block = 64

    weight = weight_row[...]
    pieces = arrived[...].astype(f32).reshape(16, 2, 8, 128)
    for half in range(2):
        turned = pieces[:, half].reshape(128, 128).T * weight
        fields[pl.ds(half * 128, 128), :] = turned
        partners[pl.ds(half * 128, 128), :] = swap_parts(turned)

    def one(r, carry):
        length = lengths[r]
        noise = (noise_one if r < half_count else noise_two).at[r % half_count]
        own = fields[pl.ds(pl.multiple_of(r * 16, 16), 16), :]
        other = partners[pl.ds(pl.multiple_of(r * 16, 16), 16), :]
        table = inner[r]
        pixel = lax.broadcasted_iota(jnp.int32, (8, SPLIT), 1)
        along = jnp.zeros((16, 128), f32)
        across = jnp.zeros((16, 128), f32)
        for start in range(0, outer, block):
            rows = []
            for j in range(start, start + block):
                rows.append(own * phase_cos[r, j : j + 1, :] + other * phase_sin[r, j : j + 1, :])
            sky = dot(jnp.concatenate(rows, axis=0).astype(bf16), table)
            weighted = []
            for j in range(start, start + block):
                noise_rows = noise[:, j * SPLIT : (j + 1) * SPLIT].astype(f32)
                noise_rows = jnp.where(pixel + j * SPLIT < length, noise_rows, 0.0)
                low = (j - start) * 16
                weighted.append(sky[low : low + 8] * noise_rows)
                weighted.append(sky[low + 8 : low + 16] * noise_rows)
            result = dot_t(jnp.concatenate(weighted, axis=0).astype(bf16), table)
            for j in range(start, start + block):
                piece = result[(j - start) * 16 : (j - start + 1) * 16]
                along = along + piece * phase_cos[r, j : j + 1, :]
                across = across + piece * phase_sin[r, j : j + 1, :]
        scale = weight / jnp.full((1, 128), length.astype(f32), f32)
        backs[pl.ds(pl.multiple_of(r * 16, 16), 16), :] = (along - swap_parts(across)) * scale
        return carry

    for r in range(cycles):
        one(r, 0)
    halves = [backs[pl.ds(half * 128, 128), :].T.reshape(16, 1, 8, 128) for half in range(2)]
    sent[...] = jnp.concatenate(halves, axis=1).reshape(256, 128).astype(bf16)


def adjoint_part(place, both, legendre, result, partner):
    width = result.shape[3]
    for d in range(4):
        core = place % 2
        owner = ((place // 2 + d) % 4) * 2 + (1 - core if partner else core)
        offset = pl.multiple_of(owner * width, width)
        for m in range(MO):
            result[d, m] = dot(both[m], legendre[m, :, pl.ds(offset, width)]).astype(result.dtype)


def adjoint_first_kernel(arrived, legendre, for_partner, both):
    values = arrived[...].astype(f32)
    row = lax.broadcasted_iota(jnp.int32, (256, 128), 0) & 7
    picked = [jnp.where(row == q, values, 0.0).astype(bf16) for q in range(8)]
    spread = dot(group_matrix(), jnp.concatenate(picked, axis=1))
    spread = jnp.where(diagonal_mask(), spread, 0.0).astype(bf16)
    back = dot_t(spread_matrix(), spread)
    for m in range(MO):
        plus = back[m * 32 : (m + 1) * 32]
        both[m] = jnp.concatenate([plus, spin_partner(plus)], axis=1).astype(bf16)
    adjoint_part(lax.axis_index("blk"), both, legendre, for_partner, True)


def adjoint_second_kernel(both, legendre, for_self):
    adjoint_part(lax.axis_index("blk"), both, legendre, for_self, False)


def pair_kernel(own, partner, *outs):
    outs[0][...] = own[0] + partner[0].astype(f32)
    for d in range(1, 4):
        outs[d][...] = (own[d] + partner[d].astype(f32)).astype(bf16)


def image_kernel(scale, own, one, two, three, direction, residual, prior, image, scalars):
    sums = [jnp.zeros((8, direction.shape[3]), f32) for _ in range(4)]
    for m in range(MO):
        for ri in range(2):
            for eb in range(2):
                part = eb * 2 + ri
                rows = pl.ds((ri * 2 + eb) * 8, 8)
                data = own[m, rows, :]
                for ref in (one, two, three):
                    data = data + ref[m, rows, :].astype(f32)
                value = data * scale
                for c in range(NB):
                    value = value + prior[eb, c] * direction[m, c, part : part + 1, :]
                image[m, :, part, :] = value
                d = direction[m, :, part, :]
                r = residual[m, :, part, :]
                sums[0] = sums[0] + r * r
                sums[1] = sums[1] + d * value
                sums[2] = sums[2] + r * value
                sums[3] = sums[3] + value * value
    lane = lax.broadcasted_iota(jnp.int32, (1, 128), 1)
    line = jnp.zeros((1, 128), f32)
    for i in range(4):
        total = jnp.sum(jnp.sum(sums[i], axis=0, keepdims=True), axis=1, keepdims=True)
        line = jnp.where(lane == i, total, line)
    scalars[...] = jnp.broadcast_to(line, scalars.shape)


def update_kernel(scalars, solution, residual, direction, image, solution_next, residual_next, direction_next):
    total = jnp.sum(scalars[...], axis=0, keepdims=True)
    rho, curvature, cross, norm = (total[:, i : i + 1] for i in range(4))
    alpha = rho / curvature
    rho_next = jnp.maximum(rho - 2.0 * alpha * cross + alpha * alpha * norm, 0.0)
    beta = rho_next / rho
    alpha = alpha.reshape(1, 1, 1)
    beta = beta.reshape(1, 1, 1)
    for m in range(MO):
        d = direction[m]
        fresh = residual[m] - alpha * image[m]
        solution_next[m] = solution[m] + alpha * d
        residual_next[m] = fresh
        direction_next[m] = fresh + beta * d


def shape(dims, kind):
    return jax.ShapeDtypeStruct(dims, kind)


def far(x):
    return pltpu.with_memory_space_constraint(x, pltpu.HBM)


def along_x(x, d):
    return lax.ppermute(x, "blk", [(i, ((i // 2 + d) % 4) * 2 + i % 2) for i in range(8)])


def other_core(x):
    return lax.ppermute(x, "blk", [(i, i ^ 1) for i in range(8)])


def shards(solution, residual, direction, legendre, prior_inverse, inverse_noise, cycle_length, order_list):
    width = direction.shape[3]
    cycles = cycle_length.shape[0]
    outer = inverse_noise.shape[2] // SPLIT
    coarse = pl.pallas_call(
        pack_kernel, out_shape=shape((MO, 32, width), bf16), in_specs=[VMEM], out_specs=VMEM, compiler_params=params(8), name="pack"
    )(direction)
    partner = other_core(coarse)
    near = [along_x(coarse, d) for d in (1, 3, 2)]
    held, still, streamed, inner, phase_cos, phase_sin, weight = pl.pallas_call(
        load_kernel,
        out_shape=(
            pltpu.VMEM((MO,) + legendre.shape[1:], bf16),
            pltpu.VMEM((MO, 32, 256), f32),
            pltpu.VMEM((MO, 256, 32), f32),
            pltpu.VMEM((cycles, 128, SPLIT), bf16),
            pltpu.VMEM((cycles, outer, 128), f32),
            pltpu.VMEM((cycles, outer, 128), f32),
            pltpu.VMEM((1, 128), f32),
        ),
        in_specs=[HBM, HBM, VMEM, VMEM, HBM],
        out_specs=(VMEM,) * 7,
        scratch_shapes=[
            pltpu.SMEM(cycle_length.shape, jnp.int32),
            pltpu.SMEM(order_list.shape, jnp.int32),
            pltpu.SemaphoreType.DMA((2 * MO + 2,)),
        ],
        compiler_params=params(8),
        cost_estimate=cost(4_000_000_000, 17_000_000),
        name="load",
    )(far(cycle_length), far(order_list), coarse, partner, far(legendre))
    joined = pl.pallas_call(
        join_kernel,
        out_shape=shape((3, MO, 32, width), bf16),
        in_specs=[VMEM] * 4,
        out_specs=VMEM,
        compiler_params=params(8),
        name="join",
    )(*near, still)
    noise_half = (cycles // 2,) + inverse_noise.shape[1:]
    still, streamed, noise_one = pl.pallas_call(
        synth_first_kernel,
        out_shape=(
            pltpu.VMEM((MO, 32, 256), f32),
            pltpu.VMEM((MO, 256, 32), f32),
            pltpu.VMEM(noise_half, bf16),
        ),
        in_specs=[VMEM] * 4 + [HBM],
        out_specs=(VMEM,) * 3,
        scratch_shapes=[pltpu.SemaphoreType.DMA],
        compiler_params=params(8),
        cost_estimate=cost(4_000_000_000, 1_000_000),
        name="synthesis_first",
    )(joined, held, still, streamed, far(inverse_noise))
    sent, noise_two = pl.pallas_call(
        synth_last_kernel,
        out_shape=(shape((256, 128), bf16), pltpu.VMEM(noise_half, bf16)),
        in_specs=[VMEM] * 4 + [HBM],
        out_specs=(VMEM, VMEM),
        scratch_shapes=[pltpu.SemaphoreType.DMA],
        compiler_params=params(8),
        cost_estimate=cost(3_000_000_000, 1_000_000),
        name="synthesis_last",
    )(other_core(joined), held, still, streamed, far(inverse_noise))
    arrived = lax.all_to_all(sent, "ma", split_axis=0, concat_axis=0, tiled=True)
    returned = pl.pallas_call(
        cycle_kernel,
        out_shape=shape((256, 128), bf16),
        in_specs=[SMEM] + [VMEM] * 7,
        out_specs=VMEM,
        scratch_shapes=[
            pltpu.VMEM((256, 128), f32),
            pltpu.VMEM((256, 128), f32),
            pltpu.VMEM((256, 128), f32),
        ],
        compiler_params=params(16),
        name="cycles",
    )(cycle_length, weight, arrived, noise_one, noise_two, inner, phase_cos, phase_sin)
    arrived = lax.all_to_all(returned, "ma", split_axis=0, concat_axis=0, tiled=True)
    stacked = held.reshape(MO, 512, 4096)
    for_partner, both = pl.pallas_call(
        adjoint_first_kernel,
        out_shape=(shape((4, MO, 32, width), bf16), shape((MO, 32, 512), bf16)),
        in_specs=[VMEM, VMEM],
        out_specs=(VMEM, VMEM),
        compiler_params=params(8),
        name="adjoint_first",
    )(arrived, stacked)
    from_partner = other_core(for_partner)
    for_self = pl.pallas_call(
        adjoint_second_kernel,
        out_shape=shape((4, MO, 32, width), f32),
        in_specs=[VMEM, VMEM],
        out_specs=VMEM,
        compiler_params=params(8),
        cost_estimate=cost(2_000_000_000, 8_000_000),
        name="adjoint_second",
    )(both, stacked)
    piece = shape((MO, 32, width), bf16)
    own, *partial = pl.pallas_call(
        pair_kernel,
        out_shape=(shape((MO, 32, width), f32), piece, piece, piece),
        in_specs=[VMEM] * 2,
        out_specs=(VMEM,) * 4,
        compiler_params=params(8), name="pairs",
    )(for_self, from_partner)
    others = [along_x(partial[d - 1], d) for d in (1, 3, 2)]

    scale = legendre.shape[3] / (legendre.shape[2] * lax.axis_size("blk"))
    image, scalars = pl.pallas_call(
        lambda *refs: image_kernel(scale, *refs),
        out_shape=(shape(direction.shape, f32), shape((128, 128), f32)),
        in_specs=[VMEM] * 7,
        out_specs=(VMEM,) * 2,
        compiler_params=params(8), name="image",
    )(own, *others, direction, residual, prior_inverse)
    scalars = lax.all_to_all(scalars, ("blk", "ma"), split_axis=0, concat_axis=0, tiled=True)
    state = shape(direction.shape, f32)
    return pl.pallas_call(
        update_kernel,
        out_shape=(state, state, state),
        in_specs=[VMEM] * 5,
        out_specs=(VMEM,) * 3,
        compiler_params=params(8), name="update",
    )(scalars, solution, residual, direction, image)


def solution(mesh):
    in_specs = (
        P("ma", None, None, "blk"),
        P("ma", None, None, "blk"),
        P("ma", None, None, "blk"),
        P("ma", None, "blk", None),
        P(None, None, None, "blk"),
        P(("blk", "ma"), None, None),
        P(("blk", "ma")),
        P(),
    )
    out_specs = (P("ma", None, None, "blk"), P("ma", None, None, "blk"), P("ma", None, None, "blk"))
    return jax.shard_map(shards, mesh=mesh, in_specs=in_specs, out_specs=out_specs, check_vma=False)
```

```python
import math

import numpy as np

import jax
import jax.numpy as jnp
from jax import lax
from jax.experimental import pallas as pl
from jax.experimental.pallas import tpu as pltpu
from jax.sharding import PartitionSpec as P

f32 = jnp.float32
bf16 = jnp.bfloat16

VMEM = pl.BlockSpec(memory_space=pltpu.VMEM)
SMEM = pl.BlockSpec(memory_space=pltpu.SMEM)
HBM = pl.BlockSpec(memory_space=pltpu.HBM)

MO = 4
NB = 8
SPLIT = 256
SIN_TERMS = (
    2 * math.pi,
    -((2 * math.pi) ** 3) / 6,
    (2 * math.pi) ** 5 / 120,
    -((2 * math.pi) ** 7) / 5040,
    (2 * math.pi) ** 9 / 362880,
    -((2 * math.pi) ** 11) / 39916800,
    (2 * math.pi) ** 13 / 6227020800,
)


def params(mib):
    return pltpu.CompilerParams(vmem_limit_bytes=mib * 1024 * 1024)


def cost(flops, nbytes):
    return pl.CostEstimate(flops=flops, bytes_accessed=nbytes, transcendentals=0)


def cos_turns(turns):
    folded = 0.25 - jnp.abs(turns - jnp.round(turns))
    square = folded * folded
    value = jnp.full_like(square, SIN_TERMS[-1])
    for term in SIN_TERMS[-2::-1]:
        value = value * square + term
    return value * folded


def mod_float(value, length, inverse):
    return value - jnp.floor(value * inverse) * length


def pack_kernel(direction, coarse):
    for m in range(MO):
        rows = []
        for ri in range(2):
            for eb in range(2):
                rows.append(direction[m, :, eb * 2 + ri, :])
        coarse[m] = jnp.concatenate(rows, axis=0).astype(bf16)


def make_tables(lengths, orders, inner, phase_cos, phase_sin, weight):
    cycles = inner.shape[0]
    outer = phase_cos.shape[1]
    lane = lax.broadcasted_iota(jnp.int32, (8, 128), 1)
    slot = (lane >> 3) * MO + (lane & (MO - 1))
    row = jnp.zeros((8, 128), f32)
    for i in range(orders.shape[0]):
        row = jnp.where(slot == i, orders[i].astype(f32), row)
    weight[...] = jnp.where(row[:1] == 0.0, 1.0, 2.0)
    column = jnp.broadcast_to(row[:1], (128, 128)).T
    lanes = lax.broadcasted_iota(jnp.int32, (128, SPLIT), 1).astype(f32)
    quarter = ((lax.broadcasted_iota(jnp.int32, (128, SPLIT), 0) >> 2) & 1).astype(f32) * 0.25
    column = jnp.concatenate([column] * (SPLIT // 128), axis=1) * lanes
    row = row * float(SPLIT)
    outer_index = lax.broadcasted_iota(jnp.int32, (outer, 128), 0).astype(f32)

    def one(r, carry):
        length = lengths[r].astype(f32)
        wide = jnp.full((8, 128), length, f32)
        inverse = 1.0 / wide
        inverse_block = jnp.broadcast_to(inverse[:1, :1], (128, SPLIT))
        wrapped = mod_float(column, length, inverse_block)
        inner[r] = cos_turns(wrapped * inverse_block + quarter).astype(bf16)
        base = mod_float(row, length, inverse)
        step = jnp.broadcast_to(base[:1], (outer, 128)) * outer_index
        inverse_outer = jnp.broadcast_to(inverse[:1], (outer, 128))
        turns = mod_float(step, length, inverse_outer) * inverse_outer
        phase_cos[r] = cos_turns(turns)
        phase_sin[r] = cos_turns(turns - 0.25)
        return carry

    lax.fori_loop(0, cycles, one, 0)


def spread_matrix():
    row = lax.broadcasted_iota(jnp.int32, (128, 1024), 0)
    lane = lax.broadcasted_iota(jnp.int32, (128, 1024), 1)
    m, ri, sb = row >> 5, (row >> 4) & 1, row & 15
    same = ((lane >> 9) == ri) & (((lane >> 7) & 3) == m) & ((lane & 15) == sb)
    return jnp.where(same, 1.0, 0.0).astype(bf16)


def group_matrix():
    row = lax.broadcasted_iota(jnp.int32, (256, 256), 0)
    lane = lax.broadcasted_iota(jnp.int32, (256, 256), 1)
    return jnp.where((row >> 3) == (lane >> 3), 1.0, 0.0).astype(bf16)


def diagonal_mask():
    row = lax.broadcasted_iota(jnp.int32, (256, 1024), 0)
    lane = lax.broadcasted_iota(jnp.int32, (256, 1024), 1)
    return ((lane >> 4) & 7) == (row & 7)


def dot(a, b):
    return jnp.dot(a, b, preferred_element_type=f32)


def dot_t(a, b):
    return lax.dot_general(a, b, (((1,), (1,)), ((), ())), preferred_element_type=f32)


def spin_partner(x):
    return jnp.concatenate([-x[24:32], x[16:24], x[8:16], -x[0:8]], axis=0)


def owner_of(position, slot):
    shift = (0, 1, 3, 2)[slot // 2]
    chip = (position // 2 + 4 - shift) % 4
    core = position % 2
    return chip * 2 + (core if slot % 2 == 0 else 1 - core)


def synth_sum(pieces, slots, legendre):
    width = pieces[0].shape[-1]
    still = jnp.zeros((32, 256), f32)
    streamed = jnp.zeros((256, 32), f32)
    for piece, slot in zip(pieces, slots):
        offset = pl.multiple_of(owner_of(lax.axis_index("blk"), slot) * width, width)
        minus = spin_partner(piece.astype(f32)).astype(bf16)
        still = still + dot_t(piece, legendre[0, :, pl.ds(offset, width)])
        streamed = streamed + dot_t(legendre[1, :, pl.ds(offset, width)], minus)
    return still, streamed


NEAR = (0, 1)
FIRST = (2, 4, 6)
LAST = (3, 5, 7)


def load_kernel(
    lengths_far, orders_far, own, partner, legendre, direction_far, prior_far,
    held, still, streamed, inner, phase_cos, phase_sin, weight, prior_term, lengths, orders, direction, prior, sems,
):
    small = [
        pltpu.make_async_copy(lengths_far, lengths, sems.at[2 * MO]),
        pltpu.make_async_copy(orders_far, orders, sems.at[2 * MO + 1]),
        pltpu.make_async_copy(direction_far, direction, sems.at[2 * MO + 2]),
        pltpu.make_async_copy(prior_far, prior, sems.at[2 * MO + 3]),
    ]
    for copy in small:
        copy.start()
    copies = []
    for m in range(MO):
        for t in range(2):
            copy = pltpu.make_async_copy(legendre.at[m, t], held.at[m, t], sems.at[2 * m + t])
            copy.start()
            copies.append(copy)
    for copy in small:
        copy.wait()
    make_tables(lengths, orders, inner, phase_cos, phase_sin, weight)
    for m in range(MO):
        for ri in range(2):
            for eb in range(2):
                part = eb * 2 + ri
                value = jnp.zeros((NB, direction.shape[3]), f32)
                for c in range(NB):
                    value = value + prior[eb, c] * direction[m, c, part : part + 1, :]
                prior_term[m, pl.ds((ri * 2 + eb) * 8, 8), :] = value
    for m in range(MO):
        copies[2 * m].wait()
        copies[2 * m + 1].wait()
        still[m], streamed[m] = synth_sum([own[m], partner[m]], NEAR, held.at[m])


def join_kernel(one, two, three, partial, joined):
    joined[0] = one[...]
    joined[1] = two[...]
    joined[2] = three[...]


def fetch_noise(noise, noise_held, sem, half):
    count = noise_held.shape[0]
    return pltpu.make_async_copy(noise.at[pl.ds(half * count, count)], noise_held, sem)


def synth_first_kernel(joined, held, still_near, streamed_near, noise, still, streamed, noise_held, sem):
    copy = fetch_noise(noise, noise_held, sem, 0)
    copy.start()
    for m in range(MO):
        one, two = synth_sum([joined[i, m] for i in range(3)], FIRST, held.at[m])
        still[m] = still_near[m] + one
        streamed[m] = streamed_near[m] + two
    copy.wait()


def synth_last_kernel(joined, held, still, streamed, noise, sent, noise_held, sem):
    copy = fetch_noise(noise, noise_held, sem, 1)
    copy.start()
    rows, columns = [], []
    for m in range(MO):
        one, two = synth_sum([joined[i, m] for i in range(3)], LAST, held.at[m])
        rows.append(still[m] + one)
        columns.append(streamed[m] + two)
    values = (jnp.concatenate(rows, axis=0).T + jnp.concatenate(columns, axis=1)).astype(bf16)
    spread = jnp.where(diagonal_mask(), dot(values, spread_matrix()), 0.0).astype(bf16)
    grouped = dot(group_matrix(), spread)
    row = lax.broadcasted_iota(jnp.int32, (256, 128), 0) & 7
    result = jnp.zeros((256, 128), f32)
    for q in range(8):
        result = jnp.where(row == q, grouped[:, q * 128 : (q + 1) * 128], result)
    sent[...] = result.astype(bf16)
    copy.wait()


def swap_parts(x):
    lane = lax.broadcasted_iota(jnp.int32, x.shape, 1)
    return jnp.where((lane & 4) == 0, -pltpu.roll(x, 124, 1), pltpu.roll(x, 4, 1))


def cycle_kernel(lengths, weight_row, arrived, noise_one, noise_two, inner, phase_cos, phase_sin, sent, fields, partners, backs):
    cycles = inner.shape[0]
    half_count = noise_one.shape[0]
    outer = phase_cos.shape[1]
    block = 64

    weight = weight_row[...]
    pieces = arrived[...].astype(f32).reshape(16, 2, 8, 128)
    for half in range(2):
        turned = pieces[:, half].reshape(128, 128).T * weight
        fields[pl.ds(half * 128, 128), :] = turned
        partners[pl.ds(half * 128, 128), :] = swap_parts(turned)

    def one(r, carry):
        length = lengths[r]
        noise = (noise_one if r < half_count else noise_two).at[r % half_count]
        own = fields[pl.ds(pl.multiple_of(r * 16, 16), 16), :]
        other = partners[pl.ds(pl.multiple_of(r * 16, 16), 16), :]
        table = inner[r]
        pixel = lax.broadcasted_iota(jnp.int32, (8, SPLIT), 1)
        along = jnp.zeros((16, 128), f32)
        across = jnp.zeros((16, 128), f32)
        for start in range(0, outer, block):
            rows = []
            for j in range(start, start + block):
                rows.append(own * phase_cos[r, j : j + 1, :] + other * phase_sin[r, j : j + 1, :])
            sky = dot(jnp.concatenate(rows, axis=0).astype(bf16), table)
            weighted = []
            for j in range(start, start + block):
                noise_rows = noise[:, j * SPLIT : (j + 1) * SPLIT].astype(f32)
                noise_rows = jnp.where(pixel + j * SPLIT < length, noise_rows, 0.0)
                low = (j - start) * 16
                weighted.append(sky[low : low + 8] * noise_rows)
                weighted.append(sky[low + 8 : low + 16] * noise_rows)
            result = dot_t(jnp.concatenate(weighted, axis=0).astype(bf16), table)
            for j in range(start, start + block):
                piece = result[(j - start) * 16 : (j - start + 1) * 16]
                along = along + piece * phase_cos[r, j : j + 1, :]
                across = across + piece * phase_sin[r, j : j + 1, :]
        scale = weight / jnp.full((1, 128), length.astype(f32), f32)
        backs[pl.ds(pl.multiple_of(r * 16, 16), 16), :] = (along - swap_parts(across)) * scale
        return carry

    for r in range(cycles):
        one(r, 0)
    halves = [backs[pl.ds(half * 128, 128), :].T.reshape(16, 1, 8, 128) for half in range(2)]
    sent[...] = jnp.concatenate(halves, axis=1).reshape(256, 128).astype(bf16)


def adjoint_part(place, both, legendre, result, partner):
    width = result.shape[3]
    for d in range(4):
        core = place % 2
        owner = ((place // 2 + d) % 4) * 2 + (1 - core if partner else core)
        offset = pl.multiple_of(owner * width, width)
        for m in range(MO):
            result[d, m] = dot(both[m], legendre[m, :, pl.ds(offset, width)]).astype(result.dtype)


def adjoint_first_kernel(arrived, legendre, for_partner, both):
    values = arrived[...].astype(f32)
    row = lax.broadcasted_iota(jnp.int32, (256, 128), 0) & 7
    picked = [jnp.where(row == q, values, 0.0).astype(bf16) for q in range(8)]
    spread = dot(group_matrix(), jnp.concatenate(picked, axis=1))
    spread = jnp.where(diagonal_mask(), spread, 0.0).astype(bf16)
    back = dot_t(spread_matrix(), spread)
    for m in range(MO):
        plus = back[m * 32 : (m + 1) * 32]
        both[m] = jnp.concatenate([plus, spin_partner(plus)], axis=1).astype(bf16)
    adjoint_part(lax.axis_index("blk"), both, legendre, for_partner, True)


def adjoint_second_kernel(both, legendre, for_self):
    adjoint_part(lax.axis_index("blk"), both, legendre, for_self, False)


def pair_kernel(own, partner, *outs):
    outs[0][...] = own[0] + partner[0].astype(f32)
    for d in range(1, 4):
        outs[d][...] = (own[d] + partner[d].astype(f32)).astype(bf16)


def image_kernel(scale, own, one, two, three, direction, residual, prior_term, image, scalars):
    sums = [jnp.zeros((8, direction.shape[3]), f32) for _ in range(4)]
    for m in range(MO):
        for ri in range(2):
            for eb in range(2):
                part = eb * 2 + ri
                rows = pl.ds((ri * 2 + eb) * 8, 8)
                data = own[m, rows, :]
                for ref in (one, two, three):
                    data = data + ref[m, rows, :].astype(f32)
                value = data * scale + prior_term[m, rows, :]
                image[m, :, part, :] = value
                d = direction[m, :, part, :]
                r = residual[m, :, part, :]
                sums[0] = sums[0] + r * r
                sums[1] = sums[1] + d * value
                sums[2] = sums[2] + r * value
                sums[3] = sums[3] + value * value
    lane = lax.broadcasted_iota(jnp.int32, (1, 128), 1)
    line = jnp.zeros((1, 128), f32)
    for i in range(4):
        total = jnp.sum(jnp.sum(sums[i], axis=0, keepdims=True), axis=1, keepdims=True)
        line = jnp.where(lane == i, total, line)
    scalars[...] = jnp.broadcast_to(line, scalars.shape)


def update_kernel(scalars, solution, residual, direction, image, solution_next, residual_next, direction_next):
    total = jnp.sum(scalars[...], axis=0, keepdims=True)
    rho, curvature, cross, norm = (total[:, i : i + 1] for i in range(4))
    alpha = rho / curvature
    rho_next = jnp.maximum(rho - 2.0 * alpha * cross + alpha * alpha * norm, 0.0)
    beta = rho_next / rho
    alpha = alpha.reshape(1, 1, 1)
    beta = beta.reshape(1, 1, 1)
    for m in range(MO):
        d = direction[m]
        fresh = residual[m] - alpha * image[m]
        solution_next[m] = solution[m] + alpha * d
        residual_next[m] = fresh
        direction_next[m] = fresh + beta * d


def shape(dims, kind):
    return jax.ShapeDtypeStruct(dims, kind)


def far(x):
    return pltpu.with_memory_space_constraint(x, pltpu.HBM)


def along_x(x, d):
    return lax.ppermute(x, "blk", [(i, ((i // 2 + d) % 4) * 2 + i % 2) for i in range(8)])


def other_core(x):
    return lax.ppermute(x, "blk", [(i, i ^ 1) for i in range(8)])


def shards(solution, residual, direction, legendre, prior_inverse, inverse_noise, cycle_length, order_list):
    width = direction.shape[3]
    cycles = cycle_length.shape[0]
    outer = inverse_noise.shape[2] // SPLIT
    coarse = pl.pallas_call(
        pack_kernel, out_shape=shape((MO, 32, width), bf16), in_specs=[VMEM], out_specs=VMEM, compiler_params=params(8), name="pack"
    )(direction)
    partner = other_core(coarse)
    near = [along_x(coarse, d) for d in (1, 3, 2)]
    held, still, streamed, inner, phase_cos, phase_sin, weight, prior_term = pl.pallas_call(
        load_kernel,
        out_shape=(
            pltpu.VMEM((MO,) + legendre.shape[1:], bf16),
            pltpu.VMEM((MO, 32, 256), f32),
            pltpu.VMEM((MO, 256, 32), f32),
            pltpu.VMEM((cycles, 128, SPLIT), bf16),
            pltpu.VMEM((cycles, outer, 128), f32),
            pltpu.VMEM((cycles, outer, 128), f32),
            pltpu.VMEM((1, 128), f32),
            pltpu.VMEM((MO, 32, width), f32),
        ),
        in_specs=[HBM, HBM, VMEM, VMEM] + [HBM] * 3,
        out_specs=(VMEM,) * 8,
        scratch_shapes=[
            pltpu.SMEM(cycle_length.shape, jnp.int32),
            pltpu.SMEM(order_list.shape, jnp.int32),
            pltpu.VMEM(direction.shape, f32),
            pltpu.VMEM(prior_inverse.shape, f32),
            pltpu.SemaphoreType.DMA((2 * MO + 4,)),
        ],
        compiler_params=params(8),
        cost_estimate=cost(4_000_000_000, 17_000_000),
        name="load",
    )(
        far(cycle_length),
        far(order_list),
        coarse,
        partner,
        far(legendre),
        far(direction),
        far(prior_inverse),
    )
    joined = pl.pallas_call(
        join_kernel,
        out_shape=shape((3, MO, 32, width), bf16),
        in_specs=[VMEM] * 4,
        out_specs=VMEM,
        compiler_params=params(8),
        name="join",
    )(*near, still)
    noise_half = (cycles // 2,) + inverse_noise.shape[1:]
    still, streamed, noise_one = pl.pallas_call(
        synth_first_kernel,
        out_shape=(
            pltpu.VMEM((MO, 32, 256), f32),
            pltpu.VMEM((MO, 256, 32), f32),
            pltpu.VMEM(noise_half, bf16),
        ),
        in_specs=[VMEM] * 4 + [HBM],
        out_specs=(VMEM,) * 3,
        scratch_shapes=[pltpu.SemaphoreType.DMA],
        compiler_params=params(8),
        cost_estimate=cost(4_000_000_000, 1_000_000),
        name="synthesis_first",
    )(joined, held, still, streamed, far(inverse_noise))
    sent, noise_two = pl.pallas_call(
        synth_last_kernel,
        out_shape=(shape((256, 128), bf16), pltpu.VMEM(noise_half, bf16)),
        in_specs=[VMEM] * 4 + [HBM],
        out_specs=(VMEM, VMEM),
        scratch_shapes=[pltpu.SemaphoreType.DMA],
        compiler_params=params(8),
        cost_estimate=cost(3_000_000_000, 1_000_000),
        name="synthesis_last",
    )(other_core(joined), held, still, streamed, far(inverse_noise))
    arrived = lax.all_to_all(sent, "ma", split_axis=0, concat_axis=0, tiled=True)
    returned = pl.pallas_call(
        cycle_kernel,
        out_shape=shape((256, 128), bf16),
        in_specs=[SMEM] + [VMEM] * 7,
        out_specs=VMEM,
        scratch_shapes=[
            pltpu.VMEM((256, 128), f32),
            pltpu.VMEM((256, 128), f32),
            pltpu.VMEM((256, 128), f32),
        ],
        compiler_params=params(16),
        name="cycles",
    )(cycle_length, weight, arrived, noise_one, noise_two, inner, phase_cos, phase_sin)
    arrived = lax.all_to_all(returned, "ma", split_axis=0, concat_axis=0, tiled=True)
    stacked = held.reshape(MO, 512, 4096)
    for_partner, both = pl.pallas_call(
        adjoint_first_kernel,
        out_shape=(shape((4, MO, 32, width), bf16), shape((MO, 32, 512), bf16)),
        in_specs=[VMEM, VMEM],
        out_specs=(VMEM, VMEM),
        compiler_params=params(8),
        name="adjoint_first",
    )(arrived, stacked)
    from_partner = other_core(for_partner)
    for_self = pl.pallas_call(
        adjoint_second_kernel,
        out_shape=shape((4, MO, 32, width), f32),
        in_specs=[VMEM, VMEM],
        out_specs=VMEM,
        compiler_params=params(8),
        cost_estimate=cost(2_000_000_000, 8_000_000),
        name="adjoint_second",
    )(both, stacked)
    piece = shape((MO, 32, width), bf16)
    own, *partial = pl.pallas_call(
        pair_kernel,
        out_shape=(shape((MO, 32, width), f32), piece, piece, piece),
        in_specs=[VMEM] * 2,
        out_specs=(VMEM,) * 4,
        compiler_params=params(8), name="pairs",
    )(for_self, from_partner)
    others = [along_x(partial[d - 1], d) for d in (1, 3, 2)]

    scale = legendre.shape[3] / (legendre.shape[2] * lax.axis_size("blk"))
    image, scalars = pl.pallas_call(
        lambda *refs: image_kernel(scale, *refs),
        out_shape=(shape(direction.shape, f32), shape((128, 128), f32)),
        in_specs=[VMEM] * 7,
        out_specs=(VMEM,) * 2,
        compiler_params=params(8), name="image",
    )(own, *others, direction, residual, prior_term)
    scalars = lax.all_to_all(scalars, ("blk", "ma"), split_axis=0, concat_axis=0, tiled=True)
    state = shape(direction.shape, f32)
    return pl.pallas_call(
        update_kernel,
        out_shape=(state, state, state),
        in_specs=[VMEM] * 5,
        out_specs=(VMEM,) * 3,
        compiler_params=params(8), name="update",
    )(scalars, solution, residual, direction, image)


def solution(mesh):
    in_specs = (
        P("ma", None, None, "blk"),
        P("ma", None, None, "blk"),
        P("ma", None, None, "blk"),
        P("ma", None, "blk", None),
        P(None, None, None, "blk"),
        P(("blk", "ma"), None, None),
        P(("blk", "ma")),
        P(),
    )
    out_specs = (P("ma", None, None, "blk"), P("ma", None, None, "blk"), P("ma", None, None, "blk"))
    return jax.shard_map(shards, mesh=mesh, in_specs=in_specs, out_specs=out_specs, check_vma=False)
```

```python
import math

import numpy as np

import jax
import jax.numpy as jnp
from jax import lax
from jax.experimental import pallas as pl
from jax.experimental.pallas import tpu as pltpu
from jax.sharding import PartitionSpec as P

f32 = jnp.float32
bf16 = jnp.bfloat16

VMEM = pl.BlockSpec(memory_space=pltpu.VMEM)
SMEM = pl.BlockSpec(memory_space=pltpu.SMEM)
HBM = pl.BlockSpec(memory_space=pltpu.HBM)

MO = 4
NB = 8
SPLIT = 256
SIN_TERMS = (
    2 * math.pi,
    -((2 * math.pi) ** 3) / 6,
    (2 * math.pi) ** 5 / 120,
    -((2 * math.pi) ** 7) / 5040,
    (2 * math.pi) ** 9 / 362880,
    -((2 * math.pi) ** 11) / 39916800,
    (2 * math.pi) ** 13 / 6227020800,
)


def params(mib):
    return pltpu.CompilerParams(vmem_limit_bytes=mib * 1024 * 1024)


def cost(flops, nbytes):
    return pl.CostEstimate(flops=flops, bytes_accessed=nbytes, transcendentals=0)


def cos_turns(turns):
    folded = 0.25 - jnp.abs(turns - jnp.round(turns))
    square = folded * folded
    value = jnp.full_like(square, SIN_TERMS[-1])
    for term in SIN_TERMS[-2::-1]:
        value = value * square + term
    return value * folded


def mod_float(value, length, inverse):
    return value - jnp.floor(value * inverse) * length


def pack_kernel(direction, coarse):
    for m in range(MO):
        rows = []
        for ri in range(2):
            for eb in range(2):
                rows.append(direction[m, :, eb * 2 + ri, :])
        coarse[m] = jnp.concatenate(rows, axis=0).astype(bf16)


def make_tables(lengths, orders, inner, phase_cos, phase_sin, weight):
    cycles = inner.shape[0]
    outer = phase_cos.shape[1]
    lane = lax.broadcasted_iota(jnp.int32, (8, 128), 1)
    slot = (lane >> 3) * MO + (lane & (MO - 1))
    row = jnp.zeros((8, 128), f32)
    for i in range(orders.shape[0]):
        row = jnp.where(slot == i, orders[i].astype(f32), row)
    weight[...] = jnp.where(row[:1] == 0.0, 1.0, 2.0)
    column = jnp.broadcast_to(row[:1], (128, 128)).T
    lanes = lax.broadcasted_iota(jnp.int32, (128, SPLIT), 1).astype(f32)
    quarter = ((lax.broadcasted_iota(jnp.int32, (128, SPLIT), 0) >> 2) & 1).astype(f32) * 0.25
    column = jnp.concatenate([column] * (SPLIT // 128), axis=1) * lanes
    row = row * float(SPLIT)
    outer_index = lax.broadcasted_iota(jnp.int32, (outer, 128), 0).astype(f32)

    def one(r, carry):
        length = lengths[r].astype(f32)
        wide = jnp.full((8, 128), length, f32)
        inverse = 1.0 / wide
        inverse_block = jnp.broadcast_to(inverse[:1, :1], (128, SPLIT))
        wrapped = mod_float(column, length, inverse_block)
        inner[r] = cos_turns(wrapped * inverse_block + quarter).astype(bf16)
        base = mod_float(row, length, inverse)
        step = jnp.broadcast_to(base[:1], (outer, 128)) * outer_index
        inverse_outer = jnp.broadcast_to(inverse[:1], (outer, 128))
        turns = mod_float(step, length, inverse_outer) * inverse_outer
        phase_cos[r] = cos_turns(turns)
        phase_sin[r] = cos_turns(turns - 0.25)
        return carry

    lax.fori_loop(0, cycles, one, 0)


def spread_matrix():
    row = lax.broadcasted_iota(jnp.int32, (128, 1024), 0)
    lane = lax.broadcasted_iota(jnp.int32, (128, 1024), 1)
    m, ri, sb = row >> 5, (row >> 4) & 1, row & 15
    same = ((lane >> 9) == ri) & (((lane >> 7) & 3) == m) & ((lane & 15) == sb)
    return jnp.where(same, 1.0, 0.0).astype(bf16)


def group_matrix():
    row = lax.broadcasted_iota(jnp.int32, (256, 256), 0)
    lane = lax.broadcasted_iota(jnp.int32, (256, 256), 1)
    return jnp.where((row >> 3) == (lane >> 3), 1.0, 0.0).astype(bf16)


def diagonal_mask():
    row = lax.broadcasted_iota(jnp.int32, (256, 1024), 0)
    lane = lax.broadcasted_iota(jnp.int32, (256, 1024), 1)
    return ((lane >> 4) & 7) == (row & 7)


def dot(a, b):
    return jnp.dot(a, b, preferred_element_type=f32)


def dot_t(a, b):
    return lax.dot_general(a, b, (((1,), (1,)), ((), ())), preferred_element_type=f32)


def spin_partner(x):
    return jnp.concatenate([-x[24:32], x[16:24], x[8:16], -x[0:8]], axis=0)


def owner_of(position, slot):
    shift = (0, 1, 3, 2)[slot // 2]
    chip = (position // 2 + 4 - shift) % 4
    core = position % 2
    return chip * 2 + (core if slot % 2 == 0 else 1 - core)


def synth_sum(pieces, slots, legendre):
    width = pieces[0].shape[-1]
    still = jnp.zeros((32, 256), f32)
    streamed = jnp.zeros((256, 32), f32)
    for piece, slot in zip(pieces, slots):
        offset = pl.multiple_of(owner_of(lax.axis_index("blk"), slot) * width, width)
        minus = spin_partner(piece.astype(f32)).astype(bf16)
        still = still + dot_t(piece, legendre[0, :, pl.ds(offset, width)])
        streamed = streamed + dot_t(legendre[1, :, pl.ds(offset, width)], minus)
    return still, streamed


NEAR = (0, 1)
FIRST = (2, 4, 6)
LAST = (3, 5, 7)


def load_kernel(
    lengths_far, orders_far, own, partner, legendre, direction_far, prior_far,
    held, still, streamed, inner, phase_cos, phase_sin, weight, prior_term, lengths, orders, direction, prior, sems,
):
    small = [
        pltpu.make_async_copy(lengths_far, lengths, sems.at[2 * MO]),
        pltpu.make_async_copy(orders_far, orders, sems.at[2 * MO + 1]),
        pltpu.make_async_copy(direction_far, direction, sems.at[2 * MO + 2]),
        pltpu.make_async_copy(prior_far, prior, sems.at[2 * MO + 3]),
    ]
    for copy in small:
        copy.start()
    copies = []
    for m in range(MO):
        for t in range(2):
            copy = pltpu.make_async_copy(legendre.at[m, t], held.at[m, t], sems.at[2 * m + t])
            copy.start()
            copies.append(copy)
    for copy in small:
        copy.wait()
    make_tables(lengths, orders, inner, phase_cos, phase_sin, weight)
    for m in range(MO):
        for ri in range(2):
            for eb in range(2):
                part = eb * 2 + ri
                value = jnp.zeros((NB, direction.shape[3]), f32)
                for c in range(NB):
                    value = value + prior[eb, c] * direction[m, c, part : part + 1, :]
                prior_term[m, pl.ds((ri * 2 + eb) * 8, 8), :] = value
    for m in range(MO):
        copies[2 * m].wait()
        copies[2 * m + 1].wait()
        still[m], streamed[m] = synth_sum([own[m], partner[m]], NEAR, held.at[m])


def join_kernel(one, two, three, partial, joined):
    joined[0] = one[...]
    joined[1] = two[...]
    joined[2] = three[...]


def fetch_noise(noise, noise_held, sem, half):
    count = noise_held.shape[0]
    return pltpu.make_async_copy(noise.at[pl.ds(half * count, count)], noise_held, sem)


def synth_first_kernel(joined, held, still_near, streamed_near, noise, still, streamed, noise_held, sem):
    copy = fetch_noise(noise, noise_held, sem, 0)
    copy.start()
    for m in range(MO):
        one, two = synth_sum([joined[i, m] for i in range(3)], FIRST, held.at[m])
        still[m] = still_near[m] + one
        streamed[m] = streamed_near[m] + two
    copy.wait()


def synth_last_kernel(joined, held, still, streamed, noise, sent, noise_held, sem):
    copy = fetch_noise(noise, noise_held, sem, 1)
    copy.start()
    rows, columns = [], []
    for m in range(MO):
        one, two = synth_sum([joined[i, m] for i in range(3)], LAST, held.at[m])
        rows.append(still[m] + one)
        columns.append(streamed[m] + two)
    values = (jnp.concatenate(rows, axis=0).T + jnp.concatenate(columns, axis=1)).astype(bf16)
    spread = jnp.where(diagonal_mask(), dot(values, spread_matrix()), 0.0).astype(bf16)
    grouped = dot(group_matrix(), spread)
    row = lax.broadcasted_iota(jnp.int32, (256, 128), 0) & 7
    result = jnp.zeros((256, 128), f32)
    for q in range(8):
        result = jnp.where(row == q, grouped[:, q * 128 : (q + 1) * 128], result)
    sent[...] = result.astype(bf16)
    copy.wait()


def swap_parts(x):
    lane = lax.broadcasted_iota(jnp.int32, x.shape, 1)
    return jnp.where((lane & 4) == 0, -pltpu.roll(x, 124, 1), pltpu.roll(x, 4, 1))


def cycle_kernel(lengths, weight_row, arrived, noise_one, noise_two, inner, phase_cos, phase_sin, sent, fields, partners, backs):
    cycles = inner.shape[0]
    half_count = noise_one.shape[0]
    outer = phase_cos.shape[1]
    block = 64

    weight = weight_row[...]
    pieces = arrived[...].astype(f32).reshape(16, 2, 8, 128)
    for half in range(2):
        turned = pieces[:, half].reshape(128, 128).T * weight
        fields[pl.ds(half * 128, 128), :] = turned
        partners[pl.ds(half * 128, 128), :] = swap_parts(turned)

    def one(r, carry):
        length = lengths[r]
        noise = (noise_one if r < half_count else noise_two).at[r % half_count]
        own = fields[pl.ds(pl.multiple_of(r * 16, 16), 16), :]
        other = partners[pl.ds(pl.multiple_of(r * 16, 16), 16), :]
        table = inner[r]
        pixel = lax.broadcasted_iota(jnp.int32, (8, SPLIT), 1)
        along = jnp.zeros((16, 128), f32)
        across = jnp.zeros((16, 128), f32)
        for start in range(0, outer, block):
            rows = []
            for j in range(start, start + block):
                rows.append(own * phase_cos[r, j : j + 1, :] + other * phase_sin[r, j : j + 1, :])
            sky = dot(jnp.concatenate(rows, axis=0).astype(bf16), table)
            weighted = []
            for j in range(start, start + block):
                noise_rows = noise[:, j * SPLIT : (j + 1) * SPLIT].astype(f32)
                noise_rows = jnp.where(pixel + j * SPLIT < length, noise_rows, 0.0)
                low = (j - start) * 16
                weighted.append(sky[low : low + 8] * noise_rows)
                weighted.append(sky[low + 8 : low + 16] * noise_rows)
            result = dot_t(jnp.concatenate(weighted, axis=0).astype(bf16), table)
            for j in range(start, start + block):
                piece = result[(j - start) * 16 : (j - start + 1) * 16]
                along = along + piece * phase_cos[r, j : j + 1, :]
                across = across + piece * phase_sin[r, j : j + 1, :]
        scale = weight / jnp.full((1, 128), length.astype(f32), f32)
        backs[pl.ds(pl.multiple_of(r * 16, 16), 16), :] = (along - swap_parts(across)) * scale
        return carry

    for r in range(cycles):
        one(r, 0)
    halves = [backs[pl.ds(half * 128, 128), :].T.reshape(16, 1, 8, 128) for half in range(2)]
    sent[...] = jnp.concatenate(halves, axis=1).reshape(256, 128).astype(bf16)


def adjoint_part(place, both, legendre, result, partner):
    width = result.shape[3]
    for d in range(4):
        core = place % 2
        owner = ((place // 2 + d) % 4) * 2 + (1 - core if partner else core)
        offset = pl.multiple_of(owner * width, width)
        for m in range(MO):
            result[d, m] = dot(both[m], legendre[m, :, pl.ds(offset, width)]).astype(result.dtype)


def adjoint_first_kernel(arrived, legendre, for_partner, both):
    values = arrived[...].astype(f32)
    row = lax.broadcasted_iota(jnp.int32, (256, 128), 0) & 7
    picked = [jnp.where(row == q, values, 0.0).astype(bf16) for q in range(8)]
    spread = dot(group_matrix(), jnp.concatenate(picked, axis=1))
    spread = jnp.where(diagonal_mask(), spread, 0.0).astype(bf16)
    back = dot_t(spread_matrix(), spread)
    for m in range(MO):
        plus = back[m * 32 : (m + 1) * 32]
        both[m] = jnp.concatenate([plus, spin_partner(plus)], axis=1).astype(bf16)
    adjoint_part(lax.axis_index("blk"), both, legendre, for_partner, True)


def adjoint_second_kernel(both, legendre, for_self):
    adjoint_part(lax.axis_index("blk"), both, legendre, for_self, False)


def pair_kernel(own, partner, *outs):
    outs[0][...] = own[0] + partner[0].astype(f32)
    for d in range(1, 4):
        outs[d][...] = (own[d] + partner[d].astype(f32)).astype(bf16)


def image_kernel(scale, own, one, two, three, direction, residual, prior_term, image, scalars):
    sums = [jnp.zeros((8, direction.shape[3]), f32) for _ in range(4)]
    for m in range(MO):
        for ri in range(2):
            for eb in range(2):
                part = eb * 2 + ri
                rows = pl.ds((ri * 2 + eb) * 8, 8)
                data = own[m, rows, :]
                for ref in (one, two, three):
                    data = data + ref[m, rows, :].astype(f32)
                value = data * scale + prior_term[m, rows, :]
                image[m, :, part, :] = value
                d = direction[m, :, part, :]
                r = residual[m, :, part, :]
                sums[0] = sums[0] + r * r
                sums[1] = sums[1] + d * value
                sums[2] = sums[2] + r * value
                sums[3] = sums[3] + value * value
    lane = lax.broadcasted_iota(jnp.int32, (1, 128), 1)
    line = jnp.zeros((1, 128), f32)
    for i in range(4):
        total = jnp.sum(jnp.sum(sums[i], axis=0, keepdims=True), axis=1, keepdims=True)
        line = jnp.where(lane == i, total, line)
    scalars[...] = jnp.broadcast_to(line, scalars.shape)


def update_kernel(scalars, solution, residual, direction, image, solution_next, residual_next, direction_next):
    total = jnp.sum(scalars[...], axis=0, keepdims=True)
    rho, curvature, cross, norm = (total[:, i : i + 1] for i in range(4))
    alpha = rho / curvature
    rho_next = jnp.maximum(rho - 2.0 * alpha * cross + alpha * alpha * norm, 0.0)
    beta = rho_next / rho
    alpha = alpha.reshape(1, 1, 1)
    beta = beta.reshape(1, 1, 1)
    for m in range(MO):
        d = direction[m]
        fresh = residual[m] - alpha * image[m]
        solution_next[m] = solution[m] + alpha * d
        residual_next[m] = fresh
        direction_next[m] = fresh + beta * d


def shape(dims, kind):
    return jax.ShapeDtypeStruct(dims, kind)


def far(x):
    return pltpu.with_memory_space_constraint(x, pltpu.HBM)


def along_x(x, d):
    return lax.ppermute(x, "blk", [(i, ((i // 2 + d) % 4) * 2 + i % 2) for i in range(8)])


def other_core(x):
    return lax.ppermute(x, "blk", [(i, i ^ 1) for i in range(8)])


def shards(solution, residual, direction, legendre, prior_inverse, inverse_noise, cycle_length, order_list):
    width = direction.shape[3]
    cycles = cycle_length.shape[0]
    outer = inverse_noise.shape[2] // SPLIT
    coarse = pl.pallas_call(
        pack_kernel, out_shape=shape((MO, 32, width), bf16), in_specs=[VMEM], out_specs=VMEM, compiler_params=params(8), name="pack"
    )(direction)
    partner = other_core(coarse)
    near = [along_x(coarse, d) for d in (1, 3, 2)]
    held, still, streamed, inner, phase_cos, phase_sin, weight, prior_term = pl.pallas_call(
        load_kernel,
        out_shape=(
            pltpu.VMEM((MO,) + legendre.shape[1:], bf16),
            pltpu.VMEM((MO, 32, 256), f32),
            pltpu.VMEM((MO, 256, 32), f32),
            pltpu.VMEM((cycles, 128, SPLIT), bf16),
            pltpu.VMEM((cycles, outer, 128), f32),
            pltpu.VMEM((cycles, outer, 128), f32),
            pltpu.VMEM((1, 128), f32),
            pltpu.VMEM((MO, 32, width), f32),
        ),
        in_specs=[HBM, HBM, VMEM, VMEM] + [HBM] * 3,
        out_specs=(VMEM,) * 8,
        scratch_shapes=[
            pltpu.SMEM(cycle_length.shape, jnp.int32),
            pltpu.SMEM(order_list.shape, jnp.int32),
            pltpu.VMEM(direction.shape, f32),
            pltpu.VMEM(prior_inverse.shape, f32),
            pltpu.SemaphoreType.DMA((2 * MO + 4,)),
        ],
        compiler_params=params(8),
        cost_estimate=cost(4_000_000_000, 17_000_000),
        name="load",
    )(
        far(cycle_length),
        far(order_list),
        coarse,
        partner,
        far(legendre),
        far(direction),
        far(prior_inverse),
    )
    joined = pl.pallas_call(
        join_kernel,
        out_shape=shape((3, MO, 32, width), bf16),
        in_specs=[VMEM] * 4,
        out_specs=VMEM,
        compiler_params=params(8),
        name="join",
    )(*near, still)
    noise_half = (cycles // 2,) + inverse_noise.shape[1:]
    still, streamed, noise_one = pl.pallas_call(
        synth_first_kernel,
        out_shape=(
            pltpu.VMEM((MO, 32, 256), f32),
            pltpu.VMEM((MO, 256, 32), f32),
            pltpu.VMEM(noise_half, bf16),
        ),
        in_specs=[VMEM] * 4 + [HBM],
        out_specs=(VMEM,) * 3,
        scratch_shapes=[pltpu.SemaphoreType.DMA],
        compiler_params=params(8),
        cost_estimate=cost(4_000_000_000, 1_000_000),
        name="synthesis_first",
    )(joined, held, still, streamed, far(inverse_noise))
    sent, noise_two = pl.pallas_call(
        synth_last_kernel,
        out_shape=(shape((256, 128), bf16), pltpu.VMEM(noise_half, bf16)),
        in_specs=[VMEM] * 4 + [HBM],
        out_specs=(VMEM, VMEM),
        scratch_shapes=[pltpu.SemaphoreType.DMA],
        compiler_params=params(8),
        cost_estimate=cost(3_000_000_000, 1_000_000),
        name="synthesis_last",
    )(other_core(joined), held, still, streamed, far(inverse_noise))
    arrived = lax.all_to_all(sent, "ma", split_axis=0, concat_axis=0, tiled=True)
    returned = pl.pallas_call(
        cycle_kernel,
        out_shape=shape((256, 128), bf16),
        in_specs=[SMEM] + [VMEM] * 7,
        out_specs=VMEM,
        scratch_shapes=[
            pltpu.VMEM((256, 128), f32),
            pltpu.VMEM((256, 128), f32),
            pltpu.VMEM((256, 128), f32),
        ],
        compiler_params=params(16),
        name="cycles",
    )(cycle_length, weight, arrived, noise_one, noise_two, inner, phase_cos, phase_sin)
    arrived = lax.all_to_all(returned, "ma", split_axis=0, concat_axis=0, tiled=True)
    stacked = held.reshape(MO, 512, 4096)
    for_partner, both = pl.pallas_call(
        adjoint_first_kernel,
        out_shape=(shape((4, MO, 32, width), bf16), shape((MO, 32, 512), bf16)),
        in_specs=[VMEM, VMEM],
        out_specs=(VMEM, VMEM),
        compiler_params=params(8),
        name="adjoint_first",
    )(arrived, stacked)
    from_partner = other_core(for_partner)
    for_self = pl.pallas_call(
        adjoint_second_kernel,
        out_shape=shape((4, MO, 32, width), f32),
        in_specs=[VMEM, VMEM],
        out_specs=VMEM,
        compiler_params=params(8),
        cost_estimate=cost(2_000_000_000, 8_000_000),
        name="adjoint_second",
    )(both, stacked)
    piece = shape((MO, 32, width), bf16)
    own, *partial = pl.pallas_call(
        pair_kernel,
        out_shape=(shape((MO, 32, width), f32), piece, piece, piece),
        in_specs=[VMEM] * 2,
        out_specs=(VMEM,) * 4,
        compiler_params=params(8), name="pairs",
    )(for_self, from_partner)
    others = [along_x(partial[d - 1], d) for d in (2, 1, 3)]

    scale = legendre.shape[3] / (legendre.shape[2] * lax.axis_size("blk"))
    image, scalars = pl.pallas_call(
        lambda *refs: image_kernel(scale, *refs),
        out_shape=(shape(direction.shape, f32), shape((128, 128), f32)),
        in_specs=[VMEM] * 7,
        out_specs=(VMEM,) * 2,
        compiler_params=params(8), name="image",
    )(own, *others, direction, residual, prior_term)
    scalars = lax.all_to_all(scalars, ("blk", "ma"), split_axis=0, concat_axis=0, tiled=True)
    state = shape(direction.shape, f32)
    return pl.pallas_call(
        update_kernel,
        out_shape=(state, state, state),
        in_specs=[VMEM] * 5,
        out_specs=(VMEM,) * 3,
        compiler_params=params(8), name="update",
    )(scalars, solution, residual, direction, image)


def solution(mesh):
    in_specs = (
        P("ma", None, None, "blk"),
        P("ma", None, None, "blk"),
        P("ma", None, None, "blk"),
        P("ma", None, "blk", None),
        P(None, None, None, "blk"),
        P(("blk", "ma"), None, None),
        P(("blk", "ma")),
        P(),
    )
    out_specs = (P("ma", None, None, "blk"), P("ma", None, None, "blk"), P("ma", None, None, "blk"))
    return jax.shard_map(shards, mesh=mesh, in_specs=in_specs, out_specs=out_specs, check_vma=False)
```
